32 devices in a mesh: pipe: 4 (over y, x), ctx: 4 (over z), exp: 2 (over core).
Axes of the slice: x: 2, y: 2, z: 4, core: 2. Of those that a mesh axis runs over, the one named last changes fastest.
Arguments:
- queries: bfloat16 [4, 2, 512, 4096], P('pipe', 'exp', 'ctx'), may hold values from -6 to 6
- rotated_keys_values: bfloat16 [4, 2, 512, 512], P('pipe', 'exp', 'ctx'), may hold values from -6 to 6
- residual: bfloat16 [4, 2, 512, 4096], P('pipe', 'exp', 'ctx'), may hold values from -6 to 6
- out_weight: bfloat16 [4, 4096, 4096], P('pipe', 'ctx', 'exp'), may hold values from -0.09375 to 0.09375
- norm_gain: float32 [4, 4096], P('pipe'), may hold values from 0.1 to 1.9
- in_weight: bfloat16 [4, 8, 4096, 1536], P('pipe', ('ctx', 'exp')), may hold values from -0.09375 to 0.09375
- down_weight: bfloat16 [4, 8, 768, 4096], P('pipe', ('ctx', 'exp')), may hold values from -0.15625 to 0.15625
- routes: int32 [4, 2, 512, 1], P('pipe', 'exp', 'ctx'), may hold values from 0 to 3; in each aligned block of 128 rows (0 to 127, 128 to 255, ..., all dimensions but the last counted through in order) at most 48 rows name the same one
- route_weight: float32 [4, 2, 512, 1], P('pipe', 'exp', 'ctx'), may hold values from 0.2 to 1
Outputs:
- section_out: bfloat16 [4, 2, 512, 4096], P('pipe', 'exp', 'ctx')
The draws below stay inside these ranges and needn't reach their ends.
Inputs may be any that keep to these rules, and one draw needn't show every extreme that they name: Among the 128 rows of one device (aligned blocks of 128 positions of one sequence of one section), no expert is named more than 48 times, and in every draw some expert is named exactly 48 times in some block. The routes of one token name different experts.
All inputs are finite; a program needn't handle non-finite values.
Results may differ from the reference program's by a relative error of at most 0.015.
Values may be sent and summed in bfloat16 or wider, within the bound.
No kernel may reach another device: no remote copies, remote signals or barrier semaphores. Data moves between devices by JAX's collectives and lax.ppermute only.
A program may use at most 128 MiB of HBM per device.

```python
import math
import jax
import jax.numpy as jnp
import numpy as np
from jax import lax

D = 4096
QUERY_HEADS = 32
KEY_VALUE_HEADS = 2
HEAD_SIZE = 128
FF = 1536
TOPK = 1
TOK_DEV = 128
GROUP = 2
FF_DEV = 768
EXPERTS = 4
CAP = 48
SEQUENCE_LENGTH = 512
BATCH_SEQUENCES = 2
N_PIPE = 4
N_CTX = 4
N_EXP = 2


def draw_queries(key, part):
    value_entries = jax.random.truncated_normal(jax.random.fold_in(key, 1), -6.0, 6.0, (N_PIPE, BATCH_SEQUENCES, SEQUENCE_LENGTH, QUERY_HEADS * HEAD_SIZE), jnp.float32)
    return value_entries.astype(jnp.bfloat16)


def draw_rotated_keys_values(key, part):
    value_entries = jax.random.truncated_normal(jax.random.fold_in(key, 3), -6.0, 6.0, (N_PIPE, BATCH_SEQUENCES, SEQUENCE_LENGTH, 2 * KEY_VALUE_HEADS * HEAD_SIZE), jnp.float32)
    return value_entries.astype(jnp.bfloat16)


def block_levels(key, dims, cuts, least, top_value):
    def one(dim, shards_of):
        draws = jax.random.uniform(jax.random.fold_in(jax.random.fold_in(key, 6), dim), (shards_of,), jnp.float32, least / len(cuts), top_value / len(cuts))
        return jnp.repeat(jnp.exp(draws), dims[dim] // shards_of).reshape((-1,) + (1,) * (len(dims) - dim - 1))

    level = one(*cuts[0])
    for cut in cuts[1:]:
        level = level * one(*cut)
    return level


def routed_block(key, own, number, rows, number_of, top, limit, lean):
    sequence = jax.random.permutation(key, number_of)
    packed, usual = load_shares(number_of, rows * top, limit, lean, True), load_shares(number_of, rows * top, limit, lean, False)
    places = jnp.arange(number_of)

    def named(lengths, rotation):
        used = int((lengths > 0).sum())
        fixed = max(1, used // 4)
        shifted = fixed + (places - fixed + rotation * (used - fixed)) % max(1, number_of - fixed)
        return jnp.zeros((number_of,), jnp.int32).at[sequence[jnp.where(places < fixed, places, shifted)]].set(jnp.asarray(lengths, jnp.int32))

    lengths = jnp.where(number % 4 == 0, named(packed, number // 4), named(usual, number - number // 4 - 1))
    mixed = jax.random.permutation(jax.random.fold_in(own, 3), number_of)
    source_of, taker = mixed[0:number_of // 2 * 2:2], mixed[1:number_of // 2 * 2:2]
    margin = jnp.minimum(lengths[source_of] - 1, limit - lengths[taker]) // 2
    margin = jnp.where((source_of == sequence[0]) | (taker == sequence[0]) | (lengths[taker] == 0), 0, jnp.maximum(margin, 0))
    shifted = jax.random.randint(jax.random.fold_in(own, 4), (number_of // 2,), 0, 1 << 20) % (margin + 1)
    lengths = lengths.at[source_of].add(-shifted).at[taker].add(shifted)
    items = jnp.searchsorted(jnp.cumsum(lengths), jnp.arange(rows * top), side="right").astype(jnp.int32)
    grid = items.reshape(top, rows).T
    grid = grid[jax.random.permutation(jax.random.fold_in(own, 1), rows)]
    rotation = jax.random.randint(jax.random.fold_in(own, 2), (rows, 1), 0, top)
    return jnp.take_along_axis(grid, (jnp.arange(top)[None, :] + rotation) % top, axis=1)


def load_shares(count, total, most, slope, full):
    weights = [(1 << 20) // math.isqrt(rank ** slope) + 1 for rank in range(1, count + 1)]
    largest = most if full else min(most, max(-(-total // count), total * weights[0] // sum(weights)))
    least = 1 if total - largest >= count - 1 else 0
    counts, spare = [largest] + [least] * (count - 1), total - largest - least * (count - 1)
    while spare > 0:
        candidates = [i for i in range(1, count) if counts[i] < largest] or [i for i in range(1, count) if counts[i] < most]
        whole, left = sum([weights[i] for i in candidates]), spare
        for i in candidates:
            more = min(most - counts[i], max(1, left * weights[i] // whole), spare)
            counts[i] = counts[i] + more
            spare = spare - more
    return np.array(counts)


def bell_draw(own_key, extent, deviation, bound, cuts=(), kind=jnp.bfloat16):
    loudness = block_levels(own_key, extent, cuts, -0.22, 0.18) if cuts else 1.0
    values = jax.random.normal(own_key, extent, jnp.float32) * deviation * loudness
    return jnp.minimum(jnp.maximum(values, -bound), bound).astype(kind)


def setup_inputs(seed: int = 0) -> dict:
    arg_keys = jax.random.split(jax.random.key(seed), 10)
    queries = draw_queries(jax.random.fold_in(arg_keys[9], 71), 0)
    rotated_keys_values = draw_rotated_keys_values(jax.random.fold_in(arg_keys[9], 71), 0)
    residual = bell_draw(arg_keys[2], (N_PIPE, BATCH_SEQUENCES, SEQUENCE_LENGTH, D), 1.0, 6.0, ((0, 4), (1, 2), (2, 4)))
    out_weight = bell_draw(arg_keys[3], (N_PIPE, QUERY_HEADS * HEAD_SIZE, D), (QUERY_HEADS * HEAD_SIZE) ** -0.5, 0.09375, ((0, 4), (1, 4), (2, 2)))
    norm_gain = jnp.clip(1.0 + 0.18 * jax.random.normal(arg_keys[4], (N_PIPE, D), jnp.float32), 0.1, 1.9)
    in_weight = bell_draw(arg_keys[5], (N_PIPE, EXPERTS * GROUP, D, 2 * FF_DEV), D ** -0.5, 0.09375, ((0, 4), (1, 8)))
    down_weight = bell_draw(arg_keys[6], (N_PIPE, EXPERTS * GROUP, FF_DEV, D), FF ** -0.5, 0.15625, ((0, 4), (1, 8)))
    routes_keys = jax.random.split(jax.random.fold_in(arg_keys[7], 1), N_PIPE * BATCH_SEQUENCES * SEQUENCE_LENGTH // TOK_DEV)
    routes_turns = jax.random.permutation(jax.random.fold_in(arg_keys[7], 3), N_PIPE * BATCH_SEQUENCES * SEQUENCE_LENGTH // TOK_DEV)
    routes = jax.vmap(lambda own, number: routed_block(jax.random.fold_in(arg_keys[7], 2), own, number, TOK_DEV, EXPERTS, TOPK, CAP, 2))(routes_keys, routes_turns).reshape((N_PIPE, BATCH_SEQUENCES, SEQUENCE_LENGTH, TOPK))
    route_weight = jnp.clip(0.2 + 0.8 * jax.random.uniform(arg_keys[8], (N_PIPE, BATCH_SEQUENCES, SEQUENCE_LENGTH, TOPK), jnp.float32) ** block_levels(arg_keys[8], (N_PIPE, BATCH_SEQUENCES, SEQUENCE_LENGTH, TOPK), ((0, 4), (1, 2), (2, 4)), -0.2, 0.2), 0.2, 1.0)
    return {"queries": queries, "rotated_keys_values": rotated_keys_values, "residual": residual, "out_weight": out_weight, "norm_gain": norm_gain, "in_weight": in_weight, "down_weight": down_weight, "routes": routes, "route_weight": route_weight}


def attend_sequence(query_rows, paired_rows):
    sequence_length = query_rows.shape[0]
    portion = QUERY_HEADS // KEY_VALUE_HEADS
    query_heads = query_rows.reshape(sequence_length, QUERY_HEADS, HEAD_SIZE).astype(jnp.float32)
    key_head_rows = jnp.repeat(paired_rows[:, :KEY_VALUE_HEADS * HEAD_SIZE].reshape(sequence_length, KEY_VALUE_HEADS, HEAD_SIZE), portion, axis=1).astype(jnp.float32)
    value_head_rows = jnp.repeat(paired_rows[:, KEY_VALUE_HEADS * HEAD_SIZE:].reshape(sequence_length, KEY_VALUE_HEADS, HEAD_SIZE), portion, axis=1).astype(jnp.float32)
    scores = jnp.einsum('qhd,khd->hqk', query_heads, key_head_rows) * (1.0 / math.sqrt(HEAD_SIZE))
    row_ids = lax.broadcasted_iota(jnp.int32, (sequence_length, sequence_length), 0)
    col_ids = lax.broadcasted_iota(jnp.int32, (sequence_length, sequence_length), 1)
    scores = jnp.where((col_ids <= row_ids)[None, :, :], scores, -jnp.inf)
    attention_weights = jax.nn.softmax(scores, axis=-1).astype(jnp.bfloat16)
    attended = jnp.einsum('hqk,khd->qhd', attention_weights.astype(jnp.float32), value_head_rows)
    return attended.reshape(sequence_length, QUERY_HEADS * HEAD_SIZE).astype(jnp.bfloat16)

def project_heads(attended, out_section):
    sequence_length = attended.shape[0]
    group_width = QUERY_HEADS * HEAD_SIZE // N_CTX
    head_groups = attended.reshape(sequence_length, N_CTX, group_width).astype(jnp.float32)
    weight_groups = out_section.reshape(N_CTX, group_width, D).astype(jnp.float32)
    head_terms = jnp.einsum('lcf,cfd->cld', head_groups, weight_groups)
    head_terms = lax.optimization_barrier(head_terms.astype(jnp.bfloat16)).astype(jnp.float32)
    return lax.optimization_barrier(jnp.sum(head_terms, axis=0))

def expert_section(normed, expert_ids, gate_weights, in_section, down_section):
    source_count = N_CTX * N_EXP
    route_rows = TOK_DEV * TOPK
    flat_ids = expert_ids.reshape(BATCH_SEQUENCES, N_CTX, route_rows)
    expert_hits = (flat_ids[..., None] == jnp.arange(EXPERTS, dtype=jnp.int32)).astype(jnp.int32)
    position = lax.optimization_barrier(jnp.sum((jnp.cumsum(expert_hits, axis=2) - 1) * expert_hits, axis=-1)).astype(jnp.int32)
    source = jnp.arange(N_CTX, dtype=jnp.int32)[None, :, None] * N_EXP + jnp.arange(BATCH_SEQUENCES, dtype=jnp.int32)[:, None, None]
    cell = ((flat_ids * source_count + source) * CAP + position).astype(jnp.int32)
    token_row = jnp.arange(BATCH_SEQUENCES, dtype=jnp.int32)[:, None, None] * SEQUENCE_LENGTH + jnp.arange(N_CTX, dtype=jnp.int32)[None, :, None] * TOK_DEV + jnp.arange(route_rows, dtype=jnp.int32)[None, None, :] // TOPK
    token_count = BATCH_SEQUENCES * SEQUENCE_LENGTH
    row_table = jnp.full((EXPERTS * source_count * CAP,), token_count, jnp.int32)
    row_table = row_table.at[cell.reshape(-1)].set(token_row.reshape(-1).astype(jnp.int32))
    row_table = row_table.reshape(EXPERTS, source_count * CAP)
    padded = jnp.concatenate([normed.reshape(token_count, D), jnp.zeros((1, D), normed.dtype)], axis=0)
    in_blocks = in_section.reshape(EXPERTS, GROUP, D, 2 * FF_DEV)
    down_blocks = down_section.reshape(EXPERTS, GROUP, FF_DEV, D)

    def one_expert(expert_args):
        row_index, in_parts, down_parts = expert_args
        slot_rows = padded[row_index]
        total = jnp.zeros((slot_rows.shape[0], D), jnp.float32)
        for block_index in range(GROUP):
            gate_up = jnp.dot(slot_rows, in_parts[block_index], preferred_element_type=jnp.float32)
            hidden = (jax.nn.silu(gate_up[:, :FF_DEV]) * gate_up[:, FF_DEV:]).astype(jnp.bfloat16)
            part = jnp.dot(hidden, down_parts[block_index], preferred_element_type=jnp.float32)
            part = lax.optimization_barrier(part.astype(jnp.bfloat16)).astype(jnp.float32)
            total = total + part
        return total
    expert_out = lax.map(one_expert, (row_table, in_blocks, down_blocks))
    picked = expert_out.reshape(-1, D)[cell.reshape(-1)]
    weighted = picked * gate_weights.reshape(-1)[:, None].astype(jnp.float32)
    return weighted.reshape(BATCH_SEQUENCES, N_CTX, TOK_DEV, TOPK, D).sum(axis=3).reshape(BATCH_SEQUENCES, SEQUENCE_LENGTH, D)

def reference(queries, rotated_keys_values, residual, out_weight, norm_gain, in_weight, down_weight, routes, route_weight):

    def one_section(section_args):
        query_section, pair_section, residual_section, out_section, gain_section, in_section, down_section, route_section, weight_section = section_args

        def one_sequence(sequence_args):
            query_rows, paired_rows, residual_rows = sequence_args
            attended = attend_sequence(query_rows, paired_rows)
            return residual_rows.astype(jnp.float32) + project_heads(attended, out_section)
        mixed = lax.map(one_sequence, (query_section, pair_section, residual_section))
        mean_square = lax.optimization_barrier(jnp.mean(mixed * mixed, axis=-1, keepdims=True))
        normed = (mixed * lax.rsqrt(mean_square + 1e-06) * gain_section.astype(jnp.float32)).astype(jnp.bfloat16)
        expert_mix = expert_section(normed, route_section, weight_section, in_section, down_section)
        return (mixed + expert_mix).astype(jnp.bfloat16)
    layer_out = lax.map(one_section, (queries, rotated_keys_values, residual, out_weight, norm_gain, in_weight, down_weight, routes, route_weight))
    return jnp.roll(layer_out, 1, axis=0)
```

```python
import math

import jax
import jax.numpy as jnp
from jax import lax
from jax.sharding import PartitionSpec as P

QUERY_HEADS = 32
KEY_VALUE_HEADS = 2
HEAD_SIZE = 128
DISPATCH_CHUNKS = 2
RETURN_CHUNKS = 2


def shift(value, axis, by):
    devices = lax.axis_size(axis)
    return lax.ppermute(value, axis, [(i, (i + by) % devices) for i in range(devices)])


def attend_block(query_block, key_rows, value_rows, row_ids, col_ids):
    scores = jnp.einsum(
        "qhd,kd->hqk", query_block, key_rows, preferred_element_type=jnp.float32
    ) * (1.0 / math.sqrt(HEAD_SIZE))
    scores = jnp.where((col_ids[None, :] <= row_ids[:, None])[None, :, :], scores, -jnp.inf)
    attention_weights = jax.nn.softmax(scores, axis=-1).astype(jnp.bfloat16)
    attended = jnp.einsum(
        "hqk,kd->qhd", attention_weights, value_rows, preferred_element_type=jnp.float32
    )
    return attended.astype(jnp.bfloat16)


def mixed_halves(queries, keys_values, residual, out_weight):
    contexts, exps = lax.axis_size("ctx"), lax.axis_size("exp")
    me, my_exp = lax.axis_index("ctx"), lax.axis_index("exp")
    rows = queries.shape[0]
    width = residual.shape[1]
    local_heads = QUERY_HEADS // contexts
    group_width = local_heads * HEAD_SIZE

    def pair_for(owner):
        head = owner * local_heads // (QUERY_HEADS // KEY_VALUE_HEADS)
        key = lax.dynamic_slice_in_dim(keys_values, head * HEAD_SIZE, HEAD_SIZE, 1)
        value = lax.dynamic_slice_in_dim(
            keys_values, (KEY_VALUE_HEADS + head) * HEAD_SIZE, HEAD_SIZE, 1
        )
        return jnp.concatenate([key, value], axis=1)

    def queries_for(owner):
        return lax.dynamic_slice_in_dim(queries, owner * group_width, group_width, 1)

    pairs = [pair_for(me)]
    blocks = [queries_for(me)]
    for k in range(1, contexts):
        pairs.append(shift(pair_for((me + k) % contexts), "ctx", k))
    for k in range(1, contexts):
        blocks.append(shift(queries_for((me + k) % contexts), "ctx", k))
    if exps == 2:
        weights = [out_weight, shift(out_weight, "exp", 1)]
        first = my_exp * (width // 2)
    else:
        gathered = lax.all_gather(out_weight, "exp", axis=1, tiled=True)
        weights = [gathered[:, : width // 2], gathered[:, width // 2 :]]
        first = 0
    offsets = [first, width // 2 - first]

    pair_rows = jnp.concatenate(pairs, axis=0)
    key_rows, value_rows = pair_rows[:, :HEAD_SIZE], pair_rows[:, HEAD_SIZE:]
    within = jnp.arange(rows, dtype=jnp.int32)
    origins = [(me - k) % contexts * rows for k in range(contexts)]
    col_ids = jnp.concatenate([origin + within for origin in origins])

    held = [None, None]
    for k in [*range(1, contexts), 0]:
        attended = attend_block(
            blocks[k].reshape(rows, local_heads, HEAD_SIZE),
            key_rows,
            value_rows,
            origins[k] + within,
            col_ids,
        ).reshape(rows, group_width)
        for half in range(2):
            term = jnp.dot(attended, weights[half], preferred_element_type=jnp.float32)
            if held[half] is not None:
                term = term + held[half].astype(jnp.float32)
            if k == 0:
                own = lax.dynamic_slice_in_dim(residual, offsets[half], width // 2, 1)
                held[half] = term + own.astype(jnp.float32)
            else:
                held[half] = shift(term.astype(jnp.bfloat16), "ctx", 1)
    return held, first


def on_device(
    queries,
    rotated_keys_values,
    residual,
    out_weight,
    norm_gain,
    in_weight,
    down_weight,
    routes,
    route_weight,
):
    contexts, exps = lax.axis_size("ctx"), lax.axis_size("exp")
    me, my_exp = lax.axis_index("ctx"), lax.axis_index("exp")
    token_rows = queries.shape[2]
    model_width = residual.shape[3]
    halves, first = mixed_halves(
        queries[0, 0], rotated_keys_values[0, 0], residual[0, 0], out_weight[0]
    )
    mixed_rows = jnp.concatenate(halves, axis=1)
    if exps == 2:
        mixed_rows = jnp.where(first == 0, mixed_rows, jnp.concatenate(halves[::-1], axis=1))

    mean_square = jnp.mean(mixed_rows * mixed_rows, axis=-1, keepdims=True)
    normed = (mixed_rows * lax.rsqrt(mean_square + 1e-06) * norm_gain[0]).astype(jnp.bfloat16)

    route_count = routes.shape[3]
    group_size = min(4, exps)
    per_context = exps // group_size
    experts = contexts * per_context
    capacity = min(
        token_rows,
        group_size
        * (
            (3 * token_rows * route_count + 2 * experts * group_size - 1)
            // (2 * experts * group_size)
        ),
    )
    slots = experts * capacity
    expert_ids = routes[0, 0].reshape(-1)
    expert_hits = (expert_ids[:, None] == jnp.arange(experts, dtype=jnp.int32)[None, :]).astype(
        jnp.int32
    )
    position = jnp.sum((jnp.cumsum(expert_hits, axis=0) - 1) * expert_hits, axis=1)
    distance = (expert_ids // per_context - me) % contexts
    slot_index = (distance * per_context + expert_ids % per_context) * capacity + position
    slot_index = slot_index.reshape(token_rows, route_count)
    slot_ids = jnp.arange(slots, dtype=jnp.int32)
    slot_match = sum(
        (slot_ids[:, None] == slot_index[None, :, r]).astype(jnp.bfloat16)
        for r in range(route_count)
    )
    packed = jnp.dot(slot_match, normed, preferred_element_type=jnp.float32).astype(jnp.bfloat16)
    packed = packed.reshape(contexts, per_context, capacity, model_width)

    def wanted_by(arrived, exp):
        if per_context == 1:
            return arrived[:, 0]
        return lax.dynamic_index_in_dim(arrived, exp // group_size, 1, keepdims=False)

    hidden_width = down_weight.shape[2]
    gate_up = 0.0
    step = model_width // DISPATCH_CHUNKS
    for chunk in range(DISPATCH_CHUNKS):
        part = packed[..., chunk * step : (chunk + 1) * step]
        arrived = jnp.stack(
            [part[0]] + [shift(part[k], "ctx", k) for k in range(1, contexts)], axis=0
        )
        gathered = [wanted_by(arrived, my_exp)]
        for k in range(1, exps):
            gathered.append(shift(wanted_by(arrived, (my_exp + k) % exps), "exp", k))
        slot_rows = jnp.concatenate(gathered, axis=0).reshape(-1, step)
        gate_up = gate_up + jnp.dot(
            slot_rows,
            in_weight[0, 0, chunk * step : (chunk + 1) * step],
            preferred_element_type=jnp.float32,
        )
    hidden = (jax.nn.silu(gate_up[:, :hidden_width]) * gate_up[:, hidden_width:]).astype(
        jnp.bfloat16
    )

    step = model_width // RETURN_CHUNKS
    outputs = []
    for chunk in range(RETURN_CHUNKS):
        columns = slice(chunk * step, (chunk + 1) * step)
        part = jnp.dot(hidden, down_weight[0, 0, :, columns], preferred_element_type=jnp.float32)
        part = part.reshape(exps, contexts, capacity, step)
        sums = [0.0] * per_context
        for k in range(exps):
            back = part[k]
            if k:
                back = shift(back.astype(jnp.bfloat16), "exp", -k).astype(jnp.float32)
            if per_context == 1:
                sums[0] = sums[0] + back
            else:
                place = (my_exp + k) % exps // group_size
                sums = [s + jnp.where(place == i, back, 0.0) for i, s in enumerate(sums)]
        total = jnp.stack(sums, axis=1).astype(jnp.bfloat16)
        returned = jnp.concatenate(
            [total[0]] + [shift(total[k], "ctx", -k) for k in range(1, contexts)], axis=0
        ).reshape(slots, step)
        layer = mixed_rows[:, columns]
        for r in range(route_count):
            match = (slot_ids[None, :] == slot_index[:, r, None]).astype(jnp.bfloat16)
            picked = jnp.dot(match, returned, preferred_element_type=jnp.float32)
            layer = layer + picked * route_weight[0, 0, :, r, None]
        outputs.append(shift(layer.astype(jnp.bfloat16), "pipe", 1))
    return jnp.concatenate(outputs, axis=1).reshape(1, 1, token_rows, model_width)


def solution(mesh):
    placed = (
        P("pipe", "exp", "ctx", None),
        P("pipe", "exp", "ctx", None),
        P("pipe", "exp", "ctx", None),
        P("pipe", "ctx", "exp"),
        P("pipe", None),
        P("pipe", ("ctx", "exp"), None, None),
        P("pipe", ("ctx", "exp"), None, None),
        P("pipe", "exp", "ctx", None),
        P("pipe", "exp", "ctx", None),
    )
    return jax.shard_map(
        on_device,
        mesh=mesh,
        in_specs=placed,
        out_specs=P("pipe", "exp", "ctx", None),
        check_vma=False,
    )
```

```python
import math

import jax
import jax.numpy as jnp
from jax import lax
from jax.sharding import PartitionSpec as P

QUERY_HEADS = 32
KEY_VALUE_HEADS = 2
HEAD_SIZE = 128
DISPATCH_CHUNKS = 4
RETURN_CHUNKS = 4


def shift(value, axis, by):
    devices = lax.axis_size(axis)
    return lax.ppermute(value, axis, [(i, (i + by) % devices) for i in range(devices)])


def across(value, mask, senders):
    return lax.ppermute(value, "ctx", [(i, i ^ mask) for i in senders])


def after(value, *earlier):
    return lax.optimization_barrier((value, *earlier))[0]


def attend_block(query_block, key_rows, value_rows, row_ids, col_ids):
    scores = jnp.einsum(
        "qhd,kd->hqk", query_block, key_rows, preferred_element_type=jnp.float32
    ) * (1.0 / math.sqrt(HEAD_SIZE))
    scores = jnp.where((col_ids[None, :] <= row_ids[:, None])[None, :, :], scores, -jnp.inf)
    attention_weights = jax.nn.softmax(scores, axis=-1).astype(jnp.bfloat16)
    attended = jnp.einsum(
        "hqk,kd->qhd", attention_weights, value_rows, preferred_element_type=jnp.float32
    )
    return attended.astype(jnp.bfloat16)


def mixed_halves(queries, keys_values, residual, out_weight):
    contexts, exps = lax.axis_size("ctx"), lax.axis_size("exp")
    me, my_exp = lax.axis_index("ctx"), lax.axis_index("exp")
    rows = queries.shape[0]
    width = residual.shape[1]
    local_heads = QUERY_HEADS // contexts
    group_width = local_heads * HEAD_SIZE
    line = contexts == 4

    def other(k):
        return me ^ k if line else (me + k) % contexts

    def came_from(k):
        return me ^ k if line else (me - k) % contexts

    def move(value, k):
        return across(value, k, range(4)) if line else shift(value, "ctx", k)

    def pair_for(owner):
        head = owner * local_heads // (QUERY_HEADS // KEY_VALUE_HEADS)
        key = lax.dynamic_slice_in_dim(keys_values, head * HEAD_SIZE, HEAD_SIZE, 1)
        value = lax.dynamic_slice_in_dim(
            keys_values, (KEY_VALUE_HEADS + head) * HEAD_SIZE, HEAD_SIZE, 1
        )
        return jnp.concatenate([key, value], axis=1)

    def queries_for(owner):
        return lax.dynamic_slice_in_dim(queries, owner * group_width, group_width, 1)

    pairs = [pair_for(me)]
    for k in range(1, contexts):
        pairs.append(move(pair_for(other(k)), k))
    outgoing = [queries_for(other(k)) for k in range(contexts)]
    if line:
        outer, inner = (0, 3), (1, 2)
        at_end = (me == 0) | (me == 3)
        far = across(outgoing[3], 3, outer)
        far_in = across(after(outgoing[2], far), 2, outer)
        next_out = across(after(outgoing[2], far_in), 2, inner)
        next_in = across(after(outgoing[3], far_in), 3, inner)
        near = across(after(outgoing[1], next_out, next_in), 1, range(4))
        blocks = [jnp.where(at_end, far, far_in), jnp.where(at_end, next_out, next_in), near]
        sources = [jnp.where(at_end, me ^ 3, me ^ 2), jnp.where(at_end, me ^ 2, me ^ 3), me ^ 1]
    else:
        blocks = [move(outgoing[k], k) for k in range(1, contexts)]
        sources = [came_from(k) for k in range(1, contexts)]
    blocks.append(outgoing[0])
    sources.append(me)
    if exps == 2:
        weights = [out_weight, shift(out_weight, "exp", 1)]
        first = my_exp * (width // 2)
    else:
        gathered = lax.all_gather(out_weight, "exp", axis=1, tiled=True)
        weights = [gathered[:, : width // 2], gathered[:, width // 2 :]]
        first = 0
    offsets = [first, width // 2 - first]

    pair_rows = jnp.concatenate(pairs, axis=0)
    key_rows, value_rows = pair_rows[:, :HEAD_SIZE], pair_rows[:, HEAD_SIZE:]
    within = jnp.arange(rows, dtype=jnp.int32)
    col_ids = jnp.concatenate([came_from(k) * rows + within for k in range(contexts)])

    outs, mids, ins = [[], []], [[], []], [[], []]
    held = [None, None]
    for step in range(contexts):
        attended = attend_block(
            blocks[step].reshape(rows, local_heads, HEAD_SIZE),
            key_rows,
            value_rows,
            sources[step] * rows + within,
            col_ids,
        ).reshape(rows, group_width)
        for half in range(2):
            term = jnp.dot(attended, weights[half], preferred_element_type=jnp.float32)
            if step == contexts - 1:
                own = lax.dynamic_slice_in_dim(residual, offsets[half], width // 2, 1)
                term = term + own.astype(jnp.float32)
                last = [outs[half][2], mids[half][1], ins[half][0]] if line else [held[half]]
                held[half] = sum([block.astype(jnp.float32) for block in last], term)
            elif line:
                outs[half].append(across(term.astype(jnp.bfloat16), 1, outer))
                if step < 2:
                    middle = (term + outs[half][step].astype(jnp.float32)).astype(jnp.bfloat16)
                    mids[half].append(across(middle, 3, inner))
                else:
                    back = (term + mids[half][0].astype(jnp.float32)).astype(jnp.bfloat16)
                    ins[half].append(across(back, 1, inner))
            else:
                if step:
                    term = term + held[half].astype(jnp.float32)
                held[half] = shift(term.astype(jnp.bfloat16), "ctx", 1)
    return held, first


def on_device(
    queries,
    rotated_keys_values,
    residual,
    out_weight,
    norm_gain,
    in_weight,
    down_weight,
    routes,
    route_weight,
):
    contexts, exps = lax.axis_size("ctx"), lax.axis_size("exp")
    me, my_exp = lax.axis_index("ctx"), lax.axis_index("exp")
    token_rows = queries.shape[2]
    model_width = residual.shape[3]
    halves, first = mixed_halves(
        queries[0, 0], rotated_keys_values[0, 0], residual[0, 0], out_weight[0]
    )
    mixed_rows = jnp.concatenate(halves, axis=1)
    if exps == 2:
        mixed_rows = jnp.where(first == 0, mixed_rows, jnp.concatenate(halves[::-1], axis=1))

    mean_square = jnp.mean(mixed_rows * mixed_rows, axis=-1, keepdims=True)
    normed = (mixed_rows * lax.rsqrt(mean_square + 1e-06) * norm_gain[0]).astype(jnp.bfloat16)

    route_count = routes.shape[3]
    group_size = min(4, exps)
    per_context = exps // group_size
    experts = contexts * per_context
    capacity = min(
        token_rows,
        group_size
        * (
            (3 * token_rows * route_count + 2 * experts * group_size - 1)
            // (2 * experts * group_size)
        ),
    )
    slots = experts * capacity
    expert_ids = routes[0, 0].reshape(-1)
    expert_hits = (expert_ids[:, None] == jnp.arange(experts, dtype=jnp.int32)[None, :]).astype(
        jnp.int32
    )
    position = jnp.sum((jnp.cumsum(expert_hits, axis=0) - 1) * expert_hits, axis=1)
    distance = (expert_ids // per_context - me) % contexts
    slot_index = (distance * per_context + expert_ids % per_context) * capacity + position
    slot_index = slot_index.reshape(token_rows, route_count)
    slot_ids = jnp.arange(slots, dtype=jnp.int32)
    slot_match = sum(
        (slot_ids[:, None] == slot_index[None, :, r]).astype(jnp.bfloat16)
        for r in range(route_count)
    )
    packed = jnp.dot(slot_match, normed, preferred_element_type=jnp.float32).astype(jnp.bfloat16)
    packed = packed.reshape(contexts, per_context, capacity, model_width)

    def wanted_by(arrived, exp):
        if per_context == 1:
            return arrived[:, 0]
        return lax.dynamic_index_in_dim(arrived, exp // group_size, 1, keepdims=False)

    hidden_width = down_weight.shape[2]
    gate_ups = [0.0]
    step = model_width // DISPATCH_CHUNKS
    for chunk in range(DISPATCH_CHUNKS):
        part = packed[..., chunk * step : (chunk + 1) * step]
        if chunk >= 2:
            part = after(part, gate_ups[chunk - 1])
        arrived = jnp.stack(
            [part[0]] + [shift(part[k], "ctx", k) for k in range(1, contexts)], axis=0
        )
        gathered = [wanted_by(arrived, my_exp)]
        for k in range(1, exps):
            gathered.append(shift(wanted_by(arrived, (my_exp + k) % exps), "exp", k))
        slot_rows = jnp.concatenate(gathered, axis=0).reshape(-1, step)
        gate_ups.append(
            gate_ups[-1]
            + jnp.dot(
                slot_rows,
                in_weight[0, 0, chunk * step : (chunk + 1) * step],
                preferred_element_type=jnp.float32,
            )
        )
    gate_up = gate_ups[-1]
    hidden = (jax.nn.silu(gate_up[:, :hidden_width]) * gate_up[:, hidden_width:]).astype(
        jnp.bfloat16
    )

    step = model_width // RETURN_CHUNKS
    outputs, layers = [], []
    for chunk in range(RETURN_CHUNKS):
        columns = slice(chunk * step, (chunk + 1) * step)
        part = jnp.dot(hidden, down_weight[0, 0, :, columns], preferred_element_type=jnp.float32)
        part = part.reshape(exps, contexts, capacity, step)
        sums = [0.0] * per_context
        for k in range(exps):
            back = part[k]
            if k:
                back = shift(back.astype(jnp.bfloat16), "exp", -k).astype(jnp.float32)
            if per_context == 1:
                sums[0] = sums[0] + back
            else:
                place = (my_exp + k) % exps // group_size
                sums = [s + jnp.where(place == i, back, 0.0) for i, s in enumerate(sums)]
        total = jnp.stack(sums, axis=1).astype(jnp.bfloat16)
        if chunk >= 2:
            total = after(total, layers[chunk - 2])
        returned = jnp.concatenate(
            [total[0]] + [shift(total[k], "ctx", -k) for k in range(1, contexts)], axis=0
        ).reshape(slots, step)
        layer = mixed_rows[:, columns]
        for r in range(route_count):
            match = (slot_ids[None, :] == slot_index[:, r, None]).astype(jnp.bfloat16)
            picked = jnp.dot(match, returned, preferred_element_type=jnp.float32)
            layer = layer + picked * route_weight[0, 0, :, r, None]
        layers.append(layer.astype(jnp.bfloat16))
        outputs.append(shift(layers[chunk], "pipe", 1))
    return jnp.concatenate(outputs, axis=1).reshape(1, 1, token_rows, model_width)


def solution(mesh):
    placed = (
        P("pipe", "exp", "ctx", None),
        P("pipe", "exp", "ctx", None),
        P("pipe", "exp", "ctx", None),
        P("pipe", "ctx", "exp"),
        P("pipe", None),
        P("pipe", ("ctx", "exp"), None, None),
        P("pipe", ("ctx", "exp"), None, None),
        P("pipe", "exp", "ctx", None),
        P("pipe", "exp", "ctx", None),
    )
    return jax.shard_map(
        on_device,
        mesh=mesh,
        in_specs=placed,
        out_specs=P("pipe", "exp", "ctx", None),
        check_vma=False,
    )
```

```python
import math

import jax
import jax.numpy as jnp
from jax import lax
from jax.sharding import PartitionSpec as P

QUERY_HEADS = 32
KEY_VALUE_HEADS = 2
HEAD_SIZE = 128


def shift(value, axis, by):
    devices = lax.axis_size(axis)
    return lax.ppermute(value, axis, [(i, (i + by) % devices) for i in range(devices)])


def after(value, *earlier):
    return lax.optimization_barrier((value, *earlier))[0]


def attend_block(query_block, key_rows, value_rows, row_ids, col_ids):
    scores = jnp.einsum(
        "qhd,kd->hqk", query_block, key_rows, preferred_element_type=jnp.float32
    ) * (1.0 / math.sqrt(HEAD_SIZE))
    scores = jnp.where((col_ids[None, :] <= row_ids[:, None])[None, :, :], scores, -jnp.inf)
    attention_weights = jax.nn.softmax(scores, axis=-1).astype(jnp.bfloat16)
    attended = jnp.einsum(
        "hqk,kd->qhd", attention_weights, value_rows, preferred_element_type=jnp.float32
    )
    return attended.astype(jnp.bfloat16)


def mixed_halves(queries, keys_values, residual, out_weight):
    contexts, exps = lax.axis_size("ctx"), lax.axis_size("exp")
    me, my_exp = lax.axis_index("ctx"), lax.axis_index("exp")
    rows = queries.shape[0]
    width = residual.shape[1]
    local_heads = QUERY_HEADS // contexts
    group_width = local_heads * HEAD_SIZE

    def pair_for(owner):
        head = owner * local_heads // (QUERY_HEADS // KEY_VALUE_HEADS)
        key = lax.dynamic_slice_in_dim(keys_values, head * HEAD_SIZE, HEAD_SIZE, 1)
        value = lax.dynamic_slice_in_dim(
            keys_values, (KEY_VALUE_HEADS + head) * HEAD_SIZE, HEAD_SIZE, 1
        )
        return jnp.concatenate([key, value], axis=1)

    def queries_for(owner):
        return lax.dynamic_slice_in_dim(queries, owner * group_width, group_width, 1)

    pairs = [pair_for(me)]
    blocks = [queries_for(me)]
    for k in range(1, contexts):
        pairs.append(shift(pair_for((me + k) % contexts), "ctx", k))
    for k in range(1, contexts):
        outgoing = queries_for((me + k) % contexts)
        if k > 1:
            outgoing = after(outgoing, blocks[1])
        blocks.append(shift(outgoing, "ctx", k))
    if exps == 2:
        weights = [out_weight, shift(out_weight, "exp", 1)]
        first = my_exp * (width // 2)
    else:
        gathered = lax.all_gather(out_weight, "exp", axis=1, tiled=True)
        weights = [gathered[:, : width // 2], gathered[:, width // 2 :]]
        first = 0
    offsets = [first, width // 2 - first]

    pair_rows = jnp.concatenate(pairs, axis=0)
    key_rows, value_rows = pair_rows[:, :HEAD_SIZE], pair_rows[:, HEAD_SIZE:]
    within = jnp.arange(rows, dtype=jnp.int32)
    origins = [(me - k) % contexts * rows for k in range(contexts)]
    col_ids = jnp.concatenate([origin + within for origin in origins])

    held, terms = [None, None], []
    for k in [*range(1, contexts), 0]:
        block = blocks[k] if k == 1 else after(blocks[k], *terms)
        attended = attend_block(
            block.reshape(rows, local_heads, HEAD_SIZE),
            key_rows,
            value_rows,
            origins[k] + within,
            col_ids,
        ).reshape(rows, group_width)
        terms = []
        for half in range(2):
            term = jnp.dot(attended, weights[half], preferred_element_type=jnp.float32)
            if k == 0:
                own = lax.dynamic_slice_in_dim(residual, offsets[half], width // 2, 1)
                term = term + own.astype(jnp.float32)
            terms.append(lax.optimization_barrier(term))
        for half in range(2):
            term = terms[half]
            if held[half] is not None:
                term = term + held[half].astype(jnp.float32)
            held[half] = term if k == 0 else shift(term.astype(jnp.bfloat16), "ctx", 1)
    return held, first


def on_device(
    queries,
    rotated_keys_values,
    residual,
    out_weight,
    norm_gain,
    in_weight,
    down_weight,
    routes,
    route_weight,
):
    contexts, exps = lax.axis_size("ctx"), lax.axis_size("exp")
    me, my_exp = lax.axis_index("ctx"), lax.axis_index("exp")
    token_rows = queries.shape[2]
    model_width = residual.shape[3]
    halves, first = mixed_halves(
        queries[0, 0], rotated_keys_values[0, 0], residual[0, 0], out_weight[0]
    )
    mixed_rows = jnp.concatenate(halves, axis=1)
    if exps == 2:
        mixed_rows = jnp.where(first == 0, mixed_rows, jnp.concatenate(halves[::-1], axis=1))

    mean_square = jnp.mean(mixed_rows * mixed_rows, axis=-1, keepdims=True)
    normed = (mixed_rows * lax.rsqrt(mean_square + 1e-06) * norm_gain[0]).astype(jnp.bfloat16)

    route_count = routes.shape[3]
    group_size = min(4, exps)
    per_context = exps // group_size
    experts = contexts * per_context
    capacity = min(
        token_rows,
        group_size
        * (
            (3 * token_rows * route_count + 2 * experts * group_size - 1)
            // (2 * experts * group_size)
        ),
    )
    slots = experts * capacity
    expert_ids = routes[0, 0].reshape(-1)
    expert_hits = (expert_ids[:, None] == jnp.arange(experts, dtype=jnp.int32)[None, :]).astype(
        jnp.int32
    )
    position = jnp.sum((jnp.cumsum(expert_hits, axis=0) - 1) * expert_hits, axis=1)
    distance = (expert_ids // per_context - me) % contexts
    slot_index = (distance * per_context + expert_ids % per_context) * capacity + position
    slot_index = slot_index.reshape(token_rows, route_count)
    slot_ids = jnp.arange(slots, dtype=jnp.int32)
    slot_match = sum(
        (slot_ids[:, None] == slot_index[None, :, r]).astype(jnp.bfloat16)
        for r in range(route_count)
    )
    next_slots = shift(slot_index.astype(jnp.float32), "pipe", 1).astype(jnp.int32)
    next_weights = shift(route_weight[0, 0], "pipe", 1)
    next_mixed = shift(mixed_rows.astype(jnp.bfloat16), "pipe", 1)
    packed = jnp.dot(slot_match, normed, preferred_element_type=jnp.float32).astype(jnp.bfloat16)
    packed = packed.reshape(contexts, per_context, capacity, model_width)

    def wanted_by(arrived, exp):
        if per_context == 1:
            return arrived[:, 0]
        return lax.dynamic_index_in_dim(arrived, exp // group_size, 1, keepdims=False)

    def exchange(arrived):
        rows = [wanted_by(arrived, my_exp)]
        for k in range(1, exps):
            rows.append(shift(wanted_by(arrived, (my_exp + k) % exps), "exp", k))
        return jnp.concatenate(rows, axis=0).reshape(-1, model_width)

    hidden_width = down_weight.shape[2]

    def expert_part(slot_rows):
        gate_up = jnp.dot(slot_rows, in_weight[0, 0], preferred_element_type=jnp.float32)
        hidden = (jax.nn.silu(gate_up[:, :hidden_width]) * gate_up[:, hidden_width:]).astype(
            jnp.bfloat16
        )
        return jnp.dot(hidden, down_weight[0, 0], preferred_element_type=jnp.float32)

    def summed(part, count):
        part = part.reshape(exps, count, capacity, model_width)
        sums = [0.0] * per_context
        for k in range(exps):
            back = part[k]
            if k:
                back = shift(back.astype(jnp.bfloat16), "exp", -k).astype(jnp.float32)
            if per_context == 1:
                sums[0] = sums[0] + back
            else:
                place = (my_exp + k) % exps // group_size
                sums = [s + jnp.where(place == i, back, 0.0) for i, s in enumerate(sums)]
        return jnp.stack(sums, axis=1).astype(jnp.bfloat16)

    def to_next_owner(rows, k):
        pipes = lax.axis_size("pipe")
        pairs = [
            (p * contexts + c, (p + 1) % pipes * contexts + (c - k) % contexts)
            for p in range(pipes)
            for c in range(contexts)
        ]
        return lax.ppermute(rows, ("pipe", "ctx"), pairs)

    order = sorted(range(1, contexts), key=lambda k: min(k, contexts - k))
    groups = [[0, order[0]]] + [[k] for k in order[1:]]
    arrived, returned = {0: packed[0]}, {}
    for place, k in enumerate(order):
        rows = packed[k]
        if place >= 2:
            rows = after(rows, arrived[order[place - 2]])
        arrived[k] = shift(rows, "ctx", k)
    part = None
    for group in groups:
        slot_rows = exchange(jnp.stack([arrived[k] for k in group], axis=0))
        if part is not None:
            slot_rows = after(slot_rows, part)
        part = expert_part(slot_rows)
        total = summed(part, len(group))
        for i, k in enumerate(group):
            returned[k] = to_next_owner(total[i], k)

    layer = next_mixed.astype(jnp.float32)
    width = per_context * capacity
    for k in [0, *order]:
        ids = slot_ids[k * width : (k + 1) * width]
        rows = returned[k].reshape(width, model_width)
        for r in range(route_count):
            match = (ids[None, :] == next_slots[:, r, None]).astype(jnp.bfloat16)
            picked = jnp.dot(match, rows, preferred_element_type=jnp.float32)
            layer = layer + picked * next_weights[:, r, None]
    return layer.astype(jnp.bfloat16).reshape(1, 1, token_rows, model_width)


def solution(mesh):
    placed = (
        P("pipe", "exp", "ctx", None),
        P("pipe", "exp", "ctx", None),
        P("pipe", "exp", "ctx", None),
        P("pipe", "ctx", "exp"),
        P("pipe", None),
        P("pipe", ("ctx", "exp"), None, None),
        P("pipe", ("ctx", "exp"), None, None),
        P("pipe", "exp", "ctx", None),
        P("pipe", "exp", "ctx", None),
    )
    return jax.shard_map(
        on_device,
        mesh=mesh,
        in_specs=placed,
        out_specs=P("pipe", "exp", "ctx", None),
        check_vma=False,
    )
```

```python
import math

import jax
import jax.numpy as jnp
from jax import lax
from jax.sharding import PartitionSpec as P

QUERY_HEADS = 32
KEY_VALUE_HEADS = 2
HEAD_SIZE = 128


def shift(value, axis, by):
    devices = lax.axis_size(axis)
    return lax.ppermute(value, axis, [(i, (i + by) % devices) for i in range(devices)])


def after(value, *earlier):
    return lax.optimization_barrier((value, *earlier))[0]


def attend_block(query_block, key_rows, value_rows, row_ids, col_ids):
    scores = jnp.einsum(
        "qhd,kd->hqk", query_block, key_rows, preferred_element_type=jnp.float32
    ) * (1.0 / math.sqrt(HEAD_SIZE))
    scores = jnp.where((col_ids[None, :] <= row_ids[:, None])[None, :, :], scores, -jnp.inf)
    attention_weights = jax.nn.softmax(scores, axis=-1).astype(jnp.bfloat16)
    attended = jnp.einsum(
        "hqk,kd->qhd", attention_weights, value_rows, preferred_element_type=jnp.float32
    )
    return attended.astype(jnp.bfloat16)


def mixed_halves(queries, keys_values, residual, out_weight, finish):
    contexts, exps = lax.axis_size("ctx"), lax.axis_size("exp")
    me, my_exp = lax.axis_index("ctx"), lax.axis_index("exp")
    rows = queries.shape[0]
    width = residual.shape[1]
    local_heads = QUERY_HEADS // contexts
    group_width = local_heads * HEAD_SIZE

    def pair_for(owner):
        head = owner * local_heads // (QUERY_HEADS // KEY_VALUE_HEADS)
        key = lax.dynamic_slice_in_dim(keys_values, head * HEAD_SIZE, HEAD_SIZE, 1)
        value = lax.dynamic_slice_in_dim(
            keys_values, (KEY_VALUE_HEADS + head) * HEAD_SIZE, HEAD_SIZE, 1
        )
        return jnp.concatenate([key, value], axis=1)

    def queries_for(owner):
        return lax.dynamic_slice_in_dim(queries, owner * group_width, group_width, 1)

    pairs = [pair_for(me)]
    blocks = [queries_for(me)]
    for k in range(1, contexts):
        pairs.append(shift(pair_for((me + k) % contexts), "ctx", k))
    for k in range(1, contexts):
        outgoing = queries_for((me + k) % contexts)
        if k > 1:
            outgoing = after(outgoing, blocks[1])
        blocks.append(shift(outgoing, "ctx", k))
    if exps == 2:
        weights = [out_weight, shift(out_weight, "exp", 1)]
        first = my_exp * (width // 2)
    else:
        gathered = lax.all_gather(out_weight, "exp", axis=1, tiled=True)
        weights = [gathered[:, : width // 2], gathered[:, width // 2 :]]
        first = 0
    offsets = [first, width // 2 - first]

    pair_rows = jnp.concatenate(pairs, axis=0)
    key_rows, value_rows = pair_rows[:, :HEAD_SIZE], pair_rows[:, HEAD_SIZE:]
    within = jnp.arange(rows, dtype=jnp.int32)
    origins = [(me - k) % contexts * rows for k in range(contexts)]
    col_ids = jnp.concatenate([origin + within for origin in origins])

    held, sent = [None, None], []
    for k in [*range(1, contexts), 0]:
        block = blocks[k] if k == 1 else after(blocks[k], *sent)
        if k == 0:
            block = after(block, finish)
        attended = attend_block(
            block.reshape(rows, local_heads, HEAD_SIZE),
            key_rows,
            value_rows,
            origins[k] + within,
            col_ids,
        ).reshape(rows, group_width)
        terms, sent = [], []
        for half in range(2):
            term = jnp.dot(attended, weights[half], preferred_element_type=jnp.float32)
            if k == 0:
                own = lax.dynamic_slice_in_dim(residual, offsets[half], width // 2, 1)
                term = term + own.astype(jnp.float32)
            terms.append(lax.optimization_barrier(term))
        for half in range(2):
            term = terms[half]
            if held[half] is not None:
                term = term + held[half].astype(jnp.float32)
            if k == 0:
                held[half] = term
            else:
                sent.append(term.astype(jnp.bfloat16))
                held[half] = shift(sent[half], "ctx", 1)
    return held, first


def on_device(
    queries,
    rotated_keys_values,
    residual,
    out_weight,
    norm_gain,
    in_weight,
    down_weight,
    routes,
    route_weight,
):
    contexts, exps = lax.axis_size("ctx"), lax.axis_size("exp")
    me, my_exp = lax.axis_index("ctx"), lax.axis_index("exp")
    token_rows = queries.shape[2]
    model_width = residual.shape[3]
    route_count = routes.shape[3]
    group_size = min(4, exps)
    per_context = exps // group_size
    experts = contexts * per_context
    capacity = min(
        token_rows,
        group_size
        * (
            (3 * token_rows * route_count + 2 * experts * group_size - 1)
            // (2 * experts * group_size)
        ),
    )
    slots = experts * capacity
    expert_ids = routes[0, 0].reshape(-1)
    expert_hits = (expert_ids[:, None] == jnp.arange(experts, dtype=jnp.int32)[None, :]).astype(
        jnp.int32
    )
    position = jnp.sum((jnp.cumsum(expert_hits, axis=0) - 1) * expert_hits, axis=1)
    distance = (expert_ids // per_context - me) % contexts
    slot_index = (distance * per_context + expert_ids % per_context) * capacity + position
    slot_index = slot_index.reshape(token_rows, route_count)
    slot_ids = jnp.arange(slots, dtype=jnp.int32)
    slot_match = sum(
        (slot_ids[:, None] == slot_index[None, :, r]).astype(jnp.bfloat16)
        for r in range(route_count)
    )
    finish = jnp.concatenate([slot_index.astype(jnp.float32).T, route_weight[0, 0].T], axis=0)
    finish = shift(finish, "pipe", 1)
    next_slots = finish[:route_count].astype(jnp.int32)
    next_weights = finish[route_count:]

    halves, first = mixed_halves(
        queries[0, 0], rotated_keys_values[0, 0], residual[0, 0], out_weight[0], finish
    )
    mixed_rows = jnp.concatenate(halves, axis=1)
    if exps == 2:
        mixed_rows = jnp.where(first == 0, mixed_rows, jnp.concatenate(halves[::-1], axis=1))

    mean_square = jnp.mean(mixed_rows * mixed_rows, axis=-1, keepdims=True)
    normed = (mixed_rows * lax.rsqrt(mean_square + 1e-06) * norm_gain[0]).astype(jnp.bfloat16)
    next_mixed = shift(mixed_rows.astype(jnp.bfloat16), "pipe", 1)
    packed = jnp.dot(slot_match, normed, preferred_element_type=jnp.float32).astype(jnp.bfloat16)
    packed = packed.reshape(contexts, per_context, capacity, model_width)

    def wanted_by(arrived, exp):
        if per_context == 1:
            return arrived[:, 0]
        return lax.dynamic_index_in_dim(arrived, exp // group_size, 1, keepdims=False)

    def exchange(arrived):
        rows = [wanted_by(arrived, my_exp)]
        for k in range(1, exps):
            rows.append(shift(wanted_by(arrived, (my_exp + k) % exps), "exp", k))
        return jnp.concatenate(rows, axis=0).reshape(-1, model_width)

    hidden_width = down_weight.shape[2]

    def expert_part(slot_rows):
        gate_up = jnp.dot(slot_rows, in_weight[0, 0], preferred_element_type=jnp.float32)
        hidden = (jax.nn.silu(gate_up[:, :hidden_width]) * gate_up[:, hidden_width:]).astype(
            jnp.bfloat16
        )
        return jnp.dot(hidden, down_weight[0, 0], preferred_element_type=jnp.float32)

    def summed(part, count):
        part = part.reshape(exps, count, capacity, model_width)
        sums = [0.0] * per_context
        for k in range(exps):
            back = part[k]
            if k:
                back = shift(back.astype(jnp.bfloat16), "exp", -k).astype(jnp.float32)
            if per_context == 1:
                sums[0] = sums[0] + back
            else:
                place = (my_exp + k) % exps // group_size
                sums = [s + jnp.where(place == i, back, 0.0) for i, s in enumerate(sums)]
        return jnp.stack(sums, axis=1).astype(jnp.bfloat16)

    def to_next_owner(rows, k):
        pipes = lax.axis_size("pipe")
        pairs = [
            (p * contexts + c, (p + 1) % pipes * contexts + (c - k) % contexts)
            for p in range(pipes)
            for c in range(contexts)
        ]
        return lax.ppermute(rows, ("pipe", "ctx"), pairs)

    order = list(range(1, contexts))
    groups = [[0, *order[:-1]], order[-1:]]
    arrived, returned = {0: packed[0]}, {}
    for k in order:
        rows = packed[k]
        if k == order[-1]:
            rows = after(rows, arrived[order[0]])
        arrived[k] = shift(rows, "ctx", k)
    total = None
    for group in groups:
        rows = jnp.stack([arrived[k] for k in group], axis=0)
        if total is not None:
            rows = after(rows, total, next_mixed)
        total = summed(expert_part(exchange(rows)), len(group))
        for i, k in enumerate(group):
            returned[k] = to_next_owner(total[i], k)

    layer = next_mixed.astype(jnp.float32)
    width = per_context * capacity
    for k in [0, *order]:
        if k == order[-1]:
            layer = lax.optimization_barrier(layer)
        ids = slot_ids[k * width : (k + 1) * width]
        rows = returned[k].reshape(width, model_width)
        for r in range(route_count):
            match = (ids[None, :] == next_slots[r, :, None]).astype(jnp.bfloat16)
            picked = jnp.dot(match, rows, preferred_element_type=jnp.float32)
            layer = layer + picked * next_weights[r, :, None]
    return layer.astype(jnp.bfloat16).reshape(1, 1, token_rows, model_width)


def solution(mesh):
    placed = (
        P("pipe", "exp", "ctx", None),
        P("pipe", "exp", "ctx", None),
        P("pipe", "exp", "ctx", None),
        P("pipe", "ctx", "exp"),
        P("pipe", None),
        P("pipe", ("ctx", "exp"), None, None),
        P("pipe", ("ctx", "exp"), None, None),
        P("pipe", "exp", "ctx", None),
        P("pipe", "exp", "ctx", None),
    )
    return jax.shard_map(
        on_device,
        mesh=mesh,
        in_specs=placed,
        out_specs=P("pipe", "exp", "ctx", None),
        check_vma=False,
    )
```

```python
import math

import jax
import jax.numpy as jnp
from jax import lax
from jax.sharding import PartitionSpec as P

QUERY_HEADS = 32
KEY_VALUE_HEADS = 2
HEAD_SIZE = 128


def shift(value, axis, by):
    devices = lax.axis_size(axis)
    return lax.ppermute(value, axis, [(i, (i + by) % devices) for i in range(devices)])


def after(value, *earlier):
    zero = sum(array.reshape(-1)[0].astype(jnp.float32) * 0.0 for array in earlier)
    return value + zero.astype(value.dtype)


def attend_block(query_block, key_rows, value_rows, row_ids, col_ids):
    scores = jnp.einsum(
        "qhd,kd->hqk", query_block, key_rows, preferred_element_type=jnp.float32
    ) * (1.0 / math.sqrt(HEAD_SIZE))
    scores = jnp.where((col_ids[None, :] <= row_ids[:, None])[None, :, :], scores, -jnp.inf)
    attention_weights = jax.nn.softmax(scores, axis=-1).astype(jnp.bfloat16)
    attended = jnp.einsum(
        "hqk,kd->qhd", attention_weights, value_rows, preferred_element_type=jnp.float32
    )
    return attended.astype(jnp.bfloat16)


def mixed_halves(queries, keys_values, residual, out_weight, finish):
    contexts, exps = lax.axis_size("ctx"), lax.axis_size("exp")
    me, my_exp = lax.axis_index("ctx"), lax.axis_index("exp")
    rows = queries.shape[0]
    width = residual.shape[1]
    local_heads = QUERY_HEADS // contexts
    group_width = local_heads * HEAD_SIZE

    def pair_for(owner):
        head = owner * local_heads // (QUERY_HEADS // KEY_VALUE_HEADS)
        key = lax.dynamic_slice_in_dim(keys_values, head * HEAD_SIZE, HEAD_SIZE, 1)
        value = lax.dynamic_slice_in_dim(
            keys_values, (KEY_VALUE_HEADS + head) * HEAD_SIZE, HEAD_SIZE, 1
        )
        return jnp.concatenate([key, value], axis=1)

    def queries_for(owner):
        return lax.dynamic_slice_in_dim(queries, owner * group_width, group_width, 1)

    pairs = [pair_for(me)]
    blocks = [queries_for(me)]
    for k in range(1, contexts):
        pairs.append(shift(pair_for((me + k) % contexts), "ctx", k))
    for k in range(1, contexts):
        outgoing = queries_for((me + k) % contexts)
        blocks.append(shift(outgoing, "ctx", k))
    if exps == 2:
        weights = [out_weight, shift(out_weight, "exp", 1)]
        first = my_exp * (width // 2)
    else:
        gathered = lax.all_gather(out_weight, "exp", axis=1, tiled=True)
        weights = [gathered[:, : width // 2], gathered[:, width // 2 :]]
        first = 0
    offsets = [first, width // 2 - first]

    pair_rows = jnp.concatenate(pairs, axis=0)
    key_rows, value_rows = pair_rows[:, :HEAD_SIZE], pair_rows[:, HEAD_SIZE:]
    within = jnp.arange(rows, dtype=jnp.int32)
    origins = [(me - k) % contexts * rows for k in range(contexts)]
    col_ids = jnp.concatenate([origin + within for origin in origins])

    held, sent = [None, None], []
    for k in [*range(1, contexts), 0]:
        block = blocks[k] if k == 1 else after(blocks[k], *sent)
        if k == 0:
            block = after(block, finish)
        attended = attend_block(
            block.reshape(rows, local_heads, HEAD_SIZE),
            key_rows,
            value_rows,
            origins[k] + within,
            col_ids,
        ).reshape(rows, group_width)
        terms, sent = [], []
        for half in range(2):
            term = jnp.dot(attended, weights[half], preferred_element_type=jnp.float32)
            if k == 0:
                own = lax.dynamic_slice_in_dim(residual, offsets[half], width // 2, 1)
                term = term + own.astype(jnp.float32)
            terms.append(lax.optimization_barrier(term))
        for half in range(2):
            term = terms[half]
            if held[half] is not None:
                term = term + held[half].astype(jnp.float32)
            if k == 0:
                held[half] = term
            else:
                sent.append(term.astype(jnp.bfloat16))
                held[half] = shift(sent[half], "ctx", 1)
    return held, first


def on_device(
    queries,
    rotated_keys_values,
    residual,
    out_weight,
    norm_gain,
    in_weight,
    down_weight,
    routes,
    route_weight,
):
    contexts, exps = lax.axis_size("ctx"), lax.axis_size("exp")
    me, my_exp = lax.axis_index("ctx"), lax.axis_index("exp")
    token_rows = queries.shape[2]
    model_width = residual.shape[3]
    route_count = routes.shape[3]
    group_size = min(4, exps)
    per_context = exps // group_size
    experts = contexts * per_context
    capacity = min(
        token_rows,
        group_size
        * (
            (3 * token_rows * route_count + 2 * experts * group_size - 1)
            // (2 * experts * group_size)
        ),
    )
    slots = experts * capacity
    expert_ids = routes[0, 0].reshape(-1)
    expert_hits = (expert_ids[:, None] == jnp.arange(experts, dtype=jnp.int32)[None, :]).astype(
        jnp.int32
    )
    position = jnp.sum((jnp.cumsum(expert_hits, axis=0) - 1) * expert_hits, axis=1)
    distance = (expert_ids // per_context - me) % contexts
    slot_index = (distance * per_context + expert_ids % per_context) * capacity + position
    slot_index = slot_index.reshape(token_rows, route_count)
    slot_ids = jnp.arange(slots, dtype=jnp.int32)
    slot_match = sum(
        (slot_ids[:, None] == slot_index[None, :, r]).astype(jnp.bfloat16)
        for r in range(route_count)
    )
    finish = jnp.concatenate([slot_index.astype(jnp.float32).T, route_weight[0, 0].T], axis=0)
    finish = shift(finish, "pipe", 1)
    next_slots = finish[:route_count].astype(jnp.int32)
    next_weights = finish[route_count:]

    halves, first = mixed_halves(
        queries[0, 0], rotated_keys_values[0, 0], residual[0, 0], out_weight[0], finish
    )
    mixed_rows = jnp.concatenate(halves, axis=1)
    if exps == 2:
        mixed_rows = jnp.where(first == 0, mixed_rows, jnp.concatenate(halves[::-1], axis=1))

    mean_square = jnp.mean(mixed_rows * mixed_rows, axis=-1, keepdims=True)
    normed = (mixed_rows * lax.rsqrt(mean_square + 1e-06) * norm_gain[0]).astype(jnp.bfloat16)
    next_mixed = shift(mixed_rows.astype(jnp.bfloat16), "pipe", 1)
    packed = jnp.dot(slot_match, normed, preferred_element_type=jnp.float32).astype(jnp.bfloat16)
    packed = packed.reshape(contexts, per_context, capacity, model_width)

    def wanted_by(arrived, exp):
        if per_context == 1:
            return arrived[:, 0]
        return lax.dynamic_index_in_dim(arrived, exp // group_size, 1, keepdims=False)

    def exchange(arrived):
        rows = [wanted_by(arrived, my_exp)]
        for k in range(1, exps):
            rows.append(shift(wanted_by(arrived, (my_exp + k) % exps), "exp", k))
        return jnp.concatenate(rows, axis=0).reshape(-1, model_width)

    hidden_width = down_weight.shape[2]

    def expert_part(slot_rows):
        gate_up = jnp.dot(slot_rows, in_weight[0, 0], preferred_element_type=jnp.float32)
        hidden = (jax.nn.silu(gate_up[:, :hidden_width]) * gate_up[:, hidden_width:]).astype(
            jnp.bfloat16
        )
        return jnp.dot(hidden, down_weight[0, 0], preferred_element_type=jnp.float32)

    def summed(part, count):
        part = part.reshape(exps, count, capacity, model_width)
        sums = [0.0] * per_context
        for k in range(exps):
            back = part[k]
            if k:
                back = shift(back.astype(jnp.bfloat16), "exp", -k).astype(jnp.float32)
            if per_context == 1:
                sums[0] = sums[0] + back
            else:
                place = (my_exp + k) % exps // group_size
                sums = [s + jnp.where(place == i, back, 0.0) for i, s in enumerate(sums)]
        return jnp.stack(sums, axis=1).astype(jnp.bfloat16)

    def to_next_owner(rows, k):
        pipes = lax.axis_size("pipe")
        pairs = [
            (p * contexts + c, (p + 1) % pipes * contexts + (c - k) % contexts)
            for p in range(pipes)
            for c in range(contexts)
        ]
        return lax.ppermute(rows, ("pipe", "ctx"), pairs)

    order = list(range(1, contexts))
    groups = [[0], order[:-1], order[-1:]]
    arrived, returned, totals = {0: packed[0]}, {}, []
    for k in order[:-1]:
        arrived[k] = shift(packed[k], "ctx", k)
    for place, group in enumerate(groups):
        if place == 1:
            last = after(packed[order[-1]], arrived[1], totals[0])
            arrived[order[-1]] = shift(last, "ctx", order[-1])
        rows = jnp.stack([arrived[k] for k in group], axis=0)
        if place:
            rows = after(rows, totals[-1], next_mixed)
        totals.append(summed(expert_part(exchange(rows)), len(group)))
        for i, k in enumerate(group):
            returned[k] = to_next_owner(totals[-1][i], k)

    layer = next_mixed.astype(jnp.float32)
    width = per_context * capacity
    for k in [0, *order]:
        if k == order[-1]:
            layer = lax.optimization_barrier(layer)
        ids = slot_ids[k * width : (k + 1) * width]
        rows = returned[k].reshape(width, model_width)
        for r in range(route_count):
            match = (ids[None, :] == next_slots[r, :, None]).astype(jnp.bfloat16)
            picked = jnp.dot(match, rows, preferred_element_type=jnp.float32)
            layer = layer + picked * next_weights[r, :, None]
    return layer.astype(jnp.bfloat16).reshape(1, 1, token_rows, model_width)


def solution(mesh):
    placed = (
        P("pipe", "exp", "ctx", None),
        P("pipe", "exp", "ctx", None),
        P("pipe", "exp", "ctx", None),
        P("pipe", "ctx", "exp"),
        P("pipe", None),
        P("pipe", ("ctx", "exp"), None, None),
        P("pipe", ("ctx", "exp"), None, None),
        P("pipe", "exp", "ctx", None),
        P("pipe", "exp", "ctx", None),
    )
    return jax.shard_map(
        on_device,
        mesh=mesh,
        in_specs=placed,
        out_specs=P("pipe", "exp", "ctx", None),
        check_vma=False,
    )
```

```python
import math

import jax
import jax.numpy as jnp
from jax import lax
from jax.sharding import PartitionSpec as P

QUERY_HEADS = 32
KEY_VALUE_HEADS = 2
HEAD_SIZE = 128


def shift(value, axis, by):
    devices = lax.axis_size(axis)
    return lax.ppermute(value, axis, [(i, (i + by) % devices) for i in range(devices)])


def after(value, *earlier):
    blocks = value.reshape(-1, *value.shape[-2:])
    first = blocks[0]
    for array in earlier:
        block = array[(0,) * (array.ndim - 2)][: first.shape[0]]
        zero = block.astype(value.dtype) * 0.0
        rows = zero.shape[0]
        first = jnp.concatenate([first[:rows] + zero, first[rows:]], axis=0)
    return jnp.concatenate([first[None], blocks[1:]], axis=0).reshape(value.shape)


def attend_block(query_block, key_rows, value_rows, row_ids, col_ids):
    scores = jnp.einsum(
        "qhd,kd->hqk", query_block, key_rows, preferred_element_type=jnp.float32
    ) * (1.0 / math.sqrt(HEAD_SIZE))
    scores = jnp.where((col_ids[None, :] <= row_ids[:, None])[None, :, :], scores, -jnp.inf)
    attention_weights = jax.nn.softmax(scores, axis=-1).astype(jnp.bfloat16)
    attended = jnp.einsum(
        "hqk,kd->qhd", attention_weights, value_rows, preferred_element_type=jnp.float32
    )
    return attended.astype(jnp.bfloat16)


def mixed_halves(queries, keys_values, residual, out_weight, finish):
    contexts, exps = lax.axis_size("ctx"), lax.axis_size("exp")
    me, my_exp = lax.axis_index("ctx"), lax.axis_index("exp")
    rows = queries.shape[0]
    width = residual.shape[1]
    local_heads = QUERY_HEADS // contexts
    group_width = local_heads * HEAD_SIZE

    def pair_for(owner):
        head = owner * local_heads // (QUERY_HEADS // KEY_VALUE_HEADS)
        key = lax.dynamic_slice_in_dim(keys_values, head * HEAD_SIZE, HEAD_SIZE, 1)
        value = lax.dynamic_slice_in_dim(
            keys_values, (KEY_VALUE_HEADS + head) * HEAD_SIZE, HEAD_SIZE, 1
        )
        return jnp.concatenate([key, value], axis=1)

    def queries_for(owner):
        return lax.dynamic_slice_in_dim(queries, owner * group_width, group_width, 1)

    pairs = [pair_for(me)]
    blocks = [queries_for(me)]
    for k in range(1, contexts):
        pairs.append(shift(pair_for((me + k) % contexts), "ctx", k))
    for k in range(1, contexts):
        outgoing = queries_for((me + k) % contexts)
        blocks.append(shift(outgoing, "ctx", k))
    if exps == 2:
        weights = [out_weight, shift(out_weight, "exp", 1)]
        first = my_exp * (width // 2)
    else:
        gathered = lax.all_gather(out_weight, "exp", axis=1, tiled=True)
        weights = [gathered[:, : width // 2], gathered[:, width // 2 :]]
        first = 0
    offsets = [first, width // 2 - first]

    pair_rows = jnp.concatenate(pairs, axis=0)
    key_rows, value_rows = pair_rows[:, :HEAD_SIZE], pair_rows[:, HEAD_SIZE:]
    within = jnp.arange(rows, dtype=jnp.int32)
    origins = [(me - k) % contexts * rows for k in range(contexts)]
    col_ids = jnp.concatenate([origin + within for origin in origins])

    held = [None, None]
    for k in [*range(1, contexts), 0]:
        block = blocks[k]
        if k == 0:
            block = block + (finish[0, 0] * 0.0).astype(block.dtype)
        attended = attend_block(
            block.reshape(rows, local_heads, HEAD_SIZE),
            key_rows,
            value_rows,
            origins[k] + within,
            col_ids,
        ).reshape(rows, group_width)
        terms = []
        for half in range(2):
            term = jnp.dot(attended, weights[half], preferred_element_type=jnp.float32)
            if k == 0:
                own = lax.dynamic_slice_in_dim(residual, offsets[half], width // 2, 1)
                term = term + own.astype(jnp.float32)
            terms.append(lax.optimization_barrier(term))
        for half in range(2):
            term = terms[half]
            if held[half] is not None:
                term = term + held[half].astype(jnp.float32)
            held[half] = term if k == 0 else shift(term.astype(jnp.bfloat16), "ctx", 1)
    return held, first


def on_device(
    queries,
    rotated_keys_values,
    residual,
    out_weight,
    norm_gain,
    in_weight,
    down_weight,
    routes,
    route_weight,
):
    contexts, exps = lax.axis_size("ctx"), lax.axis_size("exp")
    me, my_exp = lax.axis_index("ctx"), lax.axis_index("exp")
    token_rows = queries.shape[2]
    model_width = residual.shape[3]
    route_count = routes.shape[3]
    group_size = min(4, exps)
    per_context = exps // group_size
    experts = contexts * per_context
    capacity = min(
        token_rows,
        group_size
        * (
            (3 * token_rows * route_count + 2 * experts * group_size - 1)
            // (2 * experts * group_size)
        ),
    )
    slots = experts * capacity
    expert_ids = routes[0, 0].reshape(-1)
    expert_hits = (expert_ids[:, None] == jnp.arange(experts, dtype=jnp.int32)[None, :]).astype(
        jnp.int32
    )
    position = jnp.sum((jnp.cumsum(expert_hits, axis=0) - 1) * expert_hits, axis=1)
    distance = (expert_ids // per_context - me) % contexts
    slot_index = (distance * per_context + expert_ids % per_context) * capacity + position
    slot_index = slot_index.reshape(token_rows, route_count)
    slot_ids = jnp.arange(slots, dtype=jnp.int32)
    slot_match = sum(
        (slot_ids[:, None] == slot_index[None, :, r]).astype(jnp.bfloat16)
        for r in range(route_count)
    )
    finish = jnp.concatenate([slot_index.astype(jnp.float32).T, route_weight[0, 0].T], axis=0)
    finish = shift(finish, "pipe", 1)
    next_slots = finish[:route_count].astype(jnp.int32)
    next_weights = finish[route_count:]

    halves, first = mixed_halves(
        queries[0, 0], rotated_keys_values[0, 0], residual[0, 0], out_weight[0], finish
    )
    mixed_rows = jnp.concatenate(halves, axis=1)
    if exps == 2:
        mixed_rows = jnp.where(first == 0, mixed_rows, jnp.concatenate(halves[::-1], axis=1))

    mean_square = jnp.mean(mixed_rows * mixed_rows, axis=-1, keepdims=True)
    normed = (mixed_rows * lax.rsqrt(mean_square + 1e-06) * norm_gain[0]).astype(jnp.bfloat16)
    cuts = [0, token_rows * 3 // 8, token_rows * 3 // 4, token_rows]
    next_mixed = [
        shift(mixed_rows[start:stop].astype(jnp.bfloat16), "pipe", 1)
        for start, stop in zip(cuts, cuts[1:])
    ]
    packed = jnp.dot(slot_match, normed, preferred_element_type=jnp.float32).astype(jnp.bfloat16)
    packed = packed.reshape(contexts, per_context, capacity, model_width)

    def wanted_by(arrived, exp):
        if per_context == 1:
            return arrived[:, 0]
        return lax.dynamic_index_in_dim(arrived, exp // group_size, 1, keepdims=False)

    def exchange(arrived):
        rows = [wanted_by(arrived, my_exp)]
        for k in range(1, exps):
            rows.append(shift(wanted_by(arrived, (my_exp + k) % exps), "exp", k))
        return jnp.concatenate(rows, axis=0).reshape(-1, model_width)

    hidden_width = down_weight.shape[2]

    def expert_part(slot_rows):
        gate_up = jnp.dot(slot_rows, in_weight[0, 0], preferred_element_type=jnp.float32)
        hidden = (jax.nn.silu(gate_up[:, :hidden_width]) * gate_up[:, hidden_width:]).astype(
            jnp.bfloat16
        )
        return jnp.dot(hidden, down_weight[0, 0], preferred_element_type=jnp.float32)

    def summed(part, count, *earlier):
        part = part.reshape(exps, count, capacity, model_width)
        sums = [0.0] * per_context
        for k in range(exps):
            back = part[k]
            if k:
                back = after(back.astype(jnp.bfloat16), *earlier)
                back = shift(back, "exp", -k).astype(jnp.float32)
            if per_context == 1:
                sums[0] = sums[0] + back
            else:
                place = (my_exp + k) % exps // group_size
                sums = [s + jnp.where(place == i, back, 0.0) for i, s in enumerate(sums)]
        return jnp.stack(sums, axis=1).astype(jnp.bfloat16)

    def to_next_owner(rows, k):
        pipes = lax.axis_size("pipe")
        pairs = [
            (p * contexts + c, (p + 1) % pipes * contexts + (c - k) % contexts)
            for p in range(pipes)
            for c in range(contexts)
        ]
        return lax.ppermute(rows, ("pipe", "ctx"), pairs)

    order = list(range(1, contexts))
    arrived = {0: packed[0]} | {k: shift(packed[k], "ctx", k) for k in order}
    groups = [[0], order[:-1], order[-1:]]
    returned, total = {}, None
    for place, group in enumerate(groups):
        rows = jnp.stack([arrived[k] for k in group], axis=0)
        if place == 0:
            earlier = [arrived[1], next_mixed[0]]
        elif place == 1:
            rows = after(rows, returned[0], next_mixed[1])
            earlier = [arrived[order[-1]], next_mixed[2]]
        else:
            rows = after(rows, total)
            earlier = [returned[1]]
        total = summed(expert_part(exchange(rows)), len(group), *earlier)
        for i, k in enumerate(group):
            returned[k] = to_next_owner(total[i], k)

    layer = jnp.concatenate(next_mixed, axis=0).astype(jnp.float32)
    width = per_context * capacity
    for k in [0, *order]:
        if k == order[-1]:
            layer = lax.optimization_barrier(layer)
        ids = slot_ids[k * width : (k + 1) * width]
        rows = returned[k].reshape(width, model_width)
        for r in range(route_count):
            match = (ids[None, :] == next_slots[r, :, None]).astype(jnp.bfloat16)
            picked = jnp.dot(match, rows, preferred_element_type=jnp.float32)
            layer = layer + picked * next_weights[r, :, None]
    return layer.astype(jnp.bfloat16).reshape(1, 1, token_rows, model_width)


def solution(mesh):
    placed = (
        P("pipe", "exp", "ctx", None),
        P("pipe", "exp", "ctx", None),
        P("pipe", "exp", "ctx", None),
        P("pipe", "ctx", "exp"),
        P("pipe", None),
        P("pipe", ("ctx", "exp"), None, None),
        P("pipe", ("ctx", "exp"), None, None),
        P("pipe", "exp", "ctx", None),
        P("pipe", "exp", "ctx", None),
    )
    return jax.shard_map(
        on_device,
        mesh=mesh,
        in_specs=placed,
        out_specs=P("pipe", "exp", "ctx", None),
        check_vma=False,
    )
```

```python
import math

import jax
import jax.numpy as jnp
from jax import lax
from jax.sharding import PartitionSpec as P

QUERY_HEADS = 32
KEY_VALUE_HEADS = 2
HEAD_SIZE = 128


def shift(value, axis, by):
    devices = lax.axis_size(axis)
    return lax.ppermute(value, axis, [(i, (i + by) % devices) for i in range(devices)])


def attend_block(query_block, key_rows, value_rows, row_ids, col_ids):
    scores = jnp.einsum(
        "qhd,kd->hqk", query_block, key_rows, preferred_element_type=jnp.float32
    ) * (1.0 / math.sqrt(HEAD_SIZE))
    scores = jnp.where((col_ids[None, :] <= row_ids[:, None])[None, :, :], scores, -jnp.inf)
    attention_weights = jax.nn.softmax(scores, axis=-1).astype(jnp.bfloat16)
    attended = jnp.einsum(
        "hqk,kd->qhd", attention_weights, value_rows, preferred_element_type=jnp.float32
    )
    return attended.astype(jnp.bfloat16)


def mixed_halves(queries, keys_values, residual, out_weight, notes, slots_here):
    contexts, exps = lax.axis_size("ctx"), lax.axis_size("exp")
    me, my_exp = lax.axis_index("ctx"), lax.axis_index("exp")
    rows = queries.shape[0]
    width = residual.shape[1]
    local_heads = QUERY_HEADS // contexts
    group_width = local_heads * HEAD_SIZE

    note_rows = -(-len(notes[0]) // 16) * 16

    def pair_for(owner, k):
        head = owner * local_heads // (QUERY_HEADS // KEY_VALUE_HEADS)
        key = lax.dynamic_slice_in_dim(keys_values, head * HEAD_SIZE, HEAD_SIZE, 1)
        value = lax.dynamic_slice_in_dim(
            keys_values, (KEY_VALUE_HEADS + head) * HEAD_SIZE, HEAD_SIZE, 1
        )
        pair = jnp.concatenate([key, value], axis=1)
        note = jnp.pad(notes[k], ((0, note_rows - len(notes[k])), (0, 2 * HEAD_SIZE - rows)))
        return jnp.concatenate([pair, note], axis=0)

    def queries_for(owner):
        return lax.dynamic_slice_in_dim(queries, owner * group_width, group_width, 1)

    pairs = [pair_for(me, 0)]
    blocks = [queries_for(me)]
    for k in range(1, contexts):
        pairs.append(shift(pair_for((me + k) % contexts, k), "ctx", k))
    for k in range(1, contexts):
        outgoing = queries_for((me + k) % contexts)
        blocks.append(shift(outgoing, "ctx", k))
    if exps == 2:
        weights = [out_weight, shift(out_weight, "exp", 1)]
        first = my_exp * (width // 2)
    else:
        gathered = lax.all_gather(out_weight, "exp", axis=1, tiled=True)
        weights = [gathered[:, : width // 2], gathered[:, width // 2 :]]
        first = 0
    offsets = [first, width // 2 - first]

    arrived_notes = [pair[rows : rows + len(notes[0]), :rows] for pair in pairs]
    pair_rows = jnp.concatenate([pair[:rows] for pair in pairs], axis=0)
    key_rows, value_rows = pair_rows[:, :HEAD_SIZE], pair_rows[:, HEAD_SIZE:]
    within = jnp.arange(rows, dtype=jnp.int32)
    origins = [(me - k) % contexts * rows for k in range(contexts)]
    col_ids = jnp.concatenate([origin + within for origin in origins])

    held, next_slots = [None, None], None
    for k in [*range(1, contexts), 0]:
        attended = attend_block(
            blocks[k].reshape(rows, local_heads, HEAD_SIZE),
            key_rows,
            value_rows,
            origins[k] + within,
            col_ids,
        ).reshape(rows, group_width)
        if k == contexts - 1:
            follows = slots_here + held[0][0, 0].astype(jnp.float32) * 0.0
            next_slots = shift(follows, "pipe", 1)
        terms = []
        for half in range(2):
            term = jnp.dot(attended, weights[half], preferred_element_type=jnp.float32)
            if k == 0:
                own = lax.dynamic_slice_in_dim(residual, offsets[half], width // 2, 1)
                term = term + own.astype(jnp.float32)
            terms.append(lax.optimization_barrier(term))
        for half in range(2):
            term = terms[half]
            if held[half] is not None:
                term = term + held[half].astype(jnp.float32)
            if k == 0:
                held[half] = term + next_slots[0, 0] * 0.0
            else:
                held[half] = shift(term.astype(jnp.bfloat16), "ctx", 1)
    return held, first, arrived_notes, next_slots.astype(jnp.int32)


def on_device(
    queries,
    rotated_keys_values,
    residual,
    out_weight,
    norm_gain,
    in_weight,
    down_weight,
    routes,
    route_weight,
):
    contexts, exps = lax.axis_size("ctx"), lax.axis_size("exp")
    me, my_exp = lax.axis_index("ctx"), lax.axis_index("exp")
    token_rows = queries.shape[2]
    model_width = residual.shape[3]
    group_size = min(4, exps)
    per_context = exps // group_size
    experts = contexts * per_context
    capacity = min(
        token_rows,
        group_size
        * ((3 * token_rows + 2 * experts * group_size - 1) // (2 * experts * group_size)),
    )
    slots = experts * capacity
    expert_ids = routes[0, 0, :, 0]
    expert_hits = (expert_ids[:, None] == jnp.arange(experts, dtype=jnp.int32)[None, :]).astype(
        jnp.int32
    )
    position = jnp.sum((jnp.cumsum(expert_hits, axis=0) - 1) * expert_hits, axis=1)
    distance = (expert_ids // per_context - me) % contexts
    slot_index = (distance * per_context + expert_ids % per_context) * capacity + position
    slot_ids = jnp.arange(slots, dtype=jnp.int32)
    slot_match = (slot_ids[:, None] == slot_index[None, :]).astype(jnp.bfloat16)
    weights = route_weight[0, 0, :, 0]
    coarse = lax.reduce_precision(weights, exponent_bits=8, mantissa_bits=7)
    notes = []
    for k in range(contexts):
        local = slot_index - k * per_context * capacity
        local = jnp.where((local >= 0) & (local < per_context * capacity), local, -1)
        note = jnp.stack([coarse, weights - coarse, local.astype(jnp.float32)], axis=0)
        notes.append(note.astype(jnp.bfloat16))

    halves, first, arrived_notes, next_slots = mixed_halves(
        queries[0, 0],
        rotated_keys_values[0, 0],
        residual[0, 0],
        out_weight[0],
        notes,
        slot_index.astype(jnp.float32)[None, :],
    )
    mixed_rows = jnp.concatenate(halves, axis=1)
    if exps == 2:
        mixed_rows = jnp.where(first == 0, mixed_rows, jnp.concatenate(halves[::-1], axis=1))

    gain = norm_gain[0]
    scaled = (mixed_rows * gain).astype(jnp.bfloat16)
    packed = jnp.dot(slot_match, scaled, preferred_element_type=jnp.float32).astype(jnp.bfloat16)
    packed = packed.reshape(contexts, per_context, capacity, model_width)
    arrived = jnp.stack(
        [packed[0]] + [shift(packed[k], "ctx", k) for k in range(1, contexts)], axis=0
    )

    here = jnp.arange(per_context * capacity, dtype=jnp.float32)
    slot_weights = []
    for note in arrived_notes:
        note = note.astype(jnp.float32)
        hits = note[2][None, :] == here[:, None]
        slot_weights.append(jnp.sum(jnp.where(hits, note[0] + note[1], 0.0), axis=1))
    slot_weights = jnp.stack(slot_weights, axis=0).reshape(contexts, per_context, capacity, 1)

    def wanted_by(blocks, exp):
        if per_context == 1:
            return blocks[:, 0]
        return lax.dynamic_index_in_dim(blocks, exp // group_size, 1, keepdims=False)

    hidden_width = down_weight.shape[2]

    def expert_part(rows):
        rows = rows.reshape(-1, model_width)
        unscaled = rows.astype(jnp.float32) / gain
        mean_square = jnp.mean(unscaled * unscaled, axis=-1, keepdims=True)
        gate_up = jnp.dot(rows, in_weight[0, 0], preferred_element_type=jnp.float32)
        gate_up = gate_up * lax.rsqrt(mean_square + 1e-06)
        hidden = (jax.nn.silu(gate_up[:, :hidden_width]) * gate_up[:, hidden_width:]).astype(
            jnp.bfloat16
        )
        return jnp.dot(hidden, down_weight[0, 0], preferred_element_type=jnp.float32)

    others = [
        shift(wanted_by(arrived, (my_exp + k) % exps), "exp", k) for k in range(1, exps)
    ]
    own_part = expert_part(wanted_by(arrived, my_exp)).reshape(contexts, capacity, model_width)
    other_parts = expert_part(jnp.concatenate(others, axis=0)).astype(jnp.bfloat16)
    other_parts = other_parts.reshape(exps - 1, contexts, capacity, model_width)
    sums = [0.0] * per_context
    for k in range(exps):
        back = shift(other_parts[k - 1], "exp", -k).astype(jnp.float32) if k else own_part
        if per_context == 1:
            sums[0] = sums[0] + back
        else:
            place = (my_exp + k) % exps // group_size
            sums = [s + jnp.where(place == i, back, 0.0) for i, s in enumerate(sums)]
    finished = (
        arrived.astype(jnp.float32) / gain + slot_weights * jnp.stack(sums, axis=1)
    ).astype(jnp.bfloat16)

    def to_next_owner(rows, k):
        pipes = lax.axis_size("pipe")
        pairs = [
            (p * contexts + c, (p + 1) % pipes * contexts + (c - k) % contexts)
            for p in range(pipes)
            for c in range(contexts)
        ]
        return lax.ppermute(rows, ("pipe", "ctx"), pairs)

    returned = jnp.concatenate(
        [to_next_owner(finished[k], k).reshape(-1, model_width) for k in range(contexts)], axis=0
    )
    next_match = (slot_ids[None, :] == next_slots[0][:, None]).astype(jnp.bfloat16)
    layer = jnp.dot(next_match, returned, preferred_element_type=jnp.float32)
    return layer.astype(jnp.bfloat16).reshape(1, 1, token_rows, model_width)


def solution(mesh):
    placed = (
        P("pipe", "exp", "ctx", None),
        P("pipe", "exp", "ctx", None),
        P("pipe", "exp", "ctx", None),
        P("pipe", "ctx", "exp"),
        P("pipe", None),
        P("pipe", ("ctx", "exp"), None, None),
        P("pipe", ("ctx", "exp"), None, None),
        P("pipe", "exp", "ctx", None),
        P("pipe", "exp", "ctx", None),
    )
    return jax.shard_map(
        on_device,
        mesh=mesh,
        in_specs=placed,
        out_specs=P("pipe", "exp", "ctx", None),
        check_vma=False,
    )
```

```python
import functools
import math

import jax
import jax.numpy as jnp
from jax import lax
from jax.experimental import pallas as pl
from jax.experimental.pallas import tpu as pltpu
from jax.sharding import PartitionSpec as P

QUERY_HEADS = 32
KEY_VALUE_HEADS = 2
HEAD_SIZE = 128


def shift(value, axis, by):
    devices = lax.axis_size(axis)
    return lax.ppermute(value, axis, [(i, (i + by) % devices) for i in range(devices)])


IN_VMEM = pl.BlockSpec(memory_space=pltpu.VMEM)
ANYWHERE = pl.BlockSpec(memory_space=pl.ANY)


def attend_kernel(heads, origins, queries, pairs, *rest):
    out = rest[-1]
    rows = queries.shape[0]
    blocks = pairs.shape[0] // rows
    row_ids = origins[0] + lax.broadcasted_iota(jnp.int32, (rows, rows), 0)
    within = lax.broadcasted_iota(jnp.int32, (rows, rows), 1)
    seen = [origins[1 + block] + within <= row_ids for block in range(blocks)]
    seen = jnp.concatenate([one.astype(jnp.float32) for one in seen], axis=1) > 0.5
    for head in range(heads):
        columns = slice(head * HEAD_SIZE, (head + 1) * HEAD_SIZE)
        scores = lax.dot_general(
            queries[:, columns],
            pairs[:, :HEAD_SIZE],
            (((1,), (1,)), ((), ())),
            preferred_element_type=jnp.float32,
        ) * (1.0 / math.sqrt(HEAD_SIZE))
        scores = jnp.where(seen, scores, -jnp.inf)
        weights = jnp.exp(scores - jnp.max(scores, axis=1, keepdims=True))
        weights = weights / jnp.sum(weights, axis=1, keepdims=True)
        out[:, columns] = jnp.dot(
            weights.astype(jnp.bfloat16),
            pairs[:, HEAD_SIZE:],
            preferred_element_type=jnp.float32,
        ).astype(jnp.bfloat16)


def attend(queries, pairs, origins, heads, *earlier):
    rows, keys = queries.shape[0], pairs.shape[0]
    return pl.pallas_call(
        functools.partial(attend_kernel, heads),
        out_shape=jax.ShapeDtypeStruct(queries.shape, jnp.bfloat16),
        in_specs=[pl.BlockSpec(memory_space=pltpu.SMEM), IN_VMEM, IN_VMEM]
        + [ANYWHERE] * len(earlier),
        out_specs=IN_VMEM,
        cost_estimate=pl.CostEstimate(
            flops=4 * heads * rows * keys * HEAD_SIZE,
            bytes_accessed=4 * queries.size + 2 * pairs.size,
            transcendentals=heads * rows * keys,
        ),
        name="attend",
    )(origins, queries, pairs, *earlier)


def hidden_kernel(rows, into, inverse_gain, *rest):
    out = rest[-1]
    depth, width = rows.shape[1], out.shape[1]
    squares = jnp.zeros((rows.shape[0], 128), jnp.float32)
    for start in range(0, depth, 128):
        columns = slice(start, start + 128)
        mixed = rows[:, columns].astype(jnp.float32) * inverse_gain[:, columns]
        squares = squares + mixed * mixed
    scale = lax.rsqrt(jnp.sum(squares, axis=1, keepdims=True) / depth + 1e-06)
    tile = 256 if width % 256 == 0 else 128

    @pl.loop(0, width // tile)
    def _(j):
        gates = pl.ds(pl.multiple_of(j * tile, tile), tile)
        ups = pl.ds(pl.multiple_of(width + j * tile, tile), tile)
        gate = jnp.dot(rows[...], into[:, gates], preferred_element_type=jnp.float32) * scale
        up = jnp.dot(rows[...], into[:, ups], preferred_element_type=jnp.float32) * scale
        out[:, gates] = (gate / (1.0 + jnp.exp(-gate)) * up).astype(jnp.bfloat16)


def hidden_units(rows, into, inverse_gain, *earlier):
    count, depth, width = rows.shape[0], into.shape[0], into.shape[1] // 2
    return pl.pallas_call(
        hidden_kernel,
        out_shape=jax.ShapeDtypeStruct((count, width), jnp.bfloat16),
        in_specs=[IN_VMEM] * 3 + [ANYWHERE] * len(earlier),
        out_specs=IN_VMEM,
        cost_estimate=pl.CostEstimate(
            flops=4 * count * depth * width,
            bytes_accessed=2 * (rows.size + into.size),
            transcendentals=count * width,
        ),
        name="hidden_units",
    )(rows, into, inverse_gain, *earlier)


def down_kernel(hidden, down, out):
    tile = 512

    @pl.loop(0, out.shape[1] // tile)
    def _(j):
        columns = pl.ds(pl.multiple_of(j * tile, tile), tile)
        out[:, columns] = jnp.dot(
            hidden[...], down[:, columns], preferred_element_type=jnp.float32
        ).astype(out.dtype)


def down_part(hidden, down, kind):
    count, depth, width = hidden.shape[0], *down.shape
    return pl.pallas_call(
        down_kernel,
        out_shape=jax.ShapeDtypeStruct((count, width), kind),
        in_specs=[IN_VMEM] * 2,
        out_specs=IN_VMEM,
        cost_estimate=pl.CostEstimate(
            flops=2 * count * depth * width, bytes_accessed=2 * down.size, transcendentals=0
        ),
        name="down_part",
    )(hidden, down)


def mixed_halves(queries, keys_values, residual, out_weight, slot_weights, slots_here):
    contexts, exps = lax.axis_size("ctx"), lax.axis_size("exp")
    me, my_exp = lax.axis_index("ctx"), lax.axis_index("exp")
    rows = queries.shape[0]
    width = residual.shape[1]
    local_heads = QUERY_HEADS // contexts
    group_width = local_heads * HEAD_SIZE

    def pair_for(owner):
        head = owner * local_heads // (QUERY_HEADS // KEY_VALUE_HEADS)
        key = lax.dynamic_slice_in_dim(keys_values, head * HEAD_SIZE, HEAD_SIZE, 1)
        value = lax.dynamic_slice_in_dim(
            keys_values, (KEY_VALUE_HEADS + head) * HEAD_SIZE, HEAD_SIZE, 1
        )
        return jnp.concatenate([key, value], axis=1)

    def queries_for(owner):
        return lax.dynamic_slice_in_dim(queries, owner * group_width, group_width, 1)

    pairs = [pair_for(me)]
    blocks = [queries_for(me)]
    for k in range(1, contexts):
        pairs.append(shift(pair_for((me + k) % contexts), "ctx", k))
    for k in range(1, contexts):
        outgoing = queries_for((me + k) % contexts)
        blocks.append(shift(outgoing, "ctx", k))
    if exps == 2:
        weights = [out_weight, shift(out_weight, "exp", 1)]
        first = my_exp * (width // 2)
    else:
        gathered = lax.all_gather(out_weight, "exp", axis=1, tiled=True)
        weights = [gathered[:, : width // 2], gathered[:, width // 2 :]]
        first = 0
    offsets = [first, width // 2 - first]

    pair_rows = jnp.concatenate(pairs, axis=0)
    origins = [(me - k) % contexts * rows for k in range(contexts)]

    held, sent, weights_here, next_slots = [None, None], [], [slot_weights[0]], None
    for k in [*range(1, contexts), 0]:
        block_origins = jnp.stack([origins[k], *origins]).astype(jnp.int32)
        attended = attend(blocks[k], pair_rows, block_origins, local_heads, *sent)
        if k == contexts - 1:
            behind = sent[1][0, 0].astype(jnp.float32) * 0.0
            next_slots = shift(slots_here + behind, "pipe", 1)
            for j in range(1, contexts):
                weights_here.append(shift(slot_weights[j] + behind, "ctx", j))
        terms = []
        for half in range(2):
            term = jnp.dot(attended, weights[half], preferred_element_type=jnp.float32)
            if k == 0:
                own = lax.dynamic_slice_in_dim(residual, offsets[half], width // 2, 1)
                term = term + own.astype(jnp.float32)
            terms.append(lax.optimization_barrier(term))
        sent = []
        for half in range(2):
            term = terms[half]
            if held[half] is not None:
                term = term + held[half].astype(jnp.float32)
            if k == 0:
                held[half] = term
            else:
                sent.append(term.astype(jnp.bfloat16))
                held[half] = shift(sent[half], "ctx", 1)
    return held, first, jnp.concatenate(weights_here, axis=0), next_slots


def on_device(
    queries,
    rotated_keys_values,
    residual,
    out_weight,
    norm_gain,
    in_weight,
    down_weight,
    routes,
    route_weight,
):
    contexts, exps = lax.axis_size("ctx"), lax.axis_size("exp")
    me, my_exp = lax.axis_index("ctx"), lax.axis_index("exp")
    token_rows = queries.shape[2]
    model_width = residual.shape[3]
    group_size = min(4, exps)
    per_context = exps // group_size
    experts = contexts * per_context
    capacity = min(
        token_rows,
        group_size
        * ((3 * token_rows + 2 * experts * group_size - 1) // (2 * experts * group_size)),
    )
    slots = experts * capacity
    expert_ids = routes[0, 0, :, 0]
    expert_hits = (expert_ids[:, None] == jnp.arange(experts, dtype=jnp.int32)[None, :]).astype(
        jnp.int32
    )
    position = jnp.sum((jnp.cumsum(expert_hits, axis=0) - 1) * expert_hits, axis=1)
    distance = (expert_ids // per_context - me) % contexts
    slot_index = (distance * per_context + expert_ids % per_context) * capacity + position
    slot_ids = jnp.arange(slots, dtype=jnp.int32)
    slot_match = (slot_ids[:, None] == slot_index[None, :]).astype(jnp.bfloat16)
    hits = slot_ids[:, None] == slot_index[None, :]
    slot_weights = jnp.sum(jnp.where(hits, route_weight[0, 0, :, 0], 0.0), axis=1)
    halves, first, arrived_weights, next_slots = mixed_halves(
        queries[0, 0],
        rotated_keys_values[0, 0],
        residual[0, 0],
        out_weight[0],
        slot_weights.reshape(contexts, 1, per_context * capacity),
        slot_index.astype(jnp.float32)[None, :],
    )
    mixed_rows = jnp.concatenate(halves, axis=1)
    if exps == 2:
        mixed_rows = jnp.where(first == 0, mixed_rows, jnp.concatenate(halves[::-1], axis=1))

    gain = norm_gain
    inverse_gain = 1.0 / gain
    beside = sum(arrived_weights[k, 0] for k in range(contexts)) + next_slots[0, 0]
    scaled = (mixed_rows * (gain + beside * 0.0)).astype(jnp.bfloat16)
    packed = jnp.dot(slot_match, scaled, preferred_element_type=jnp.float32).astype(jnp.bfloat16)
    packed = packed.reshape(contexts, per_context, capacity, model_width)
    arrived = jnp.stack(
        [packed[0]] + [shift(packed[k], "ctx", k) for k in range(1, contexts)], axis=0
    )

    def wanted_by(blocks, exp):
        if per_context == 1:
            return blocks[:, 0]
        return lax.dynamic_index_in_dim(blocks, exp // group_size, 1, keepdims=False)

    own_rows = wanted_by(arrived, my_exp).reshape(-1, model_width)
    other_rows = jnp.concatenate(
        [shift(wanted_by(arrived, (my_exp + k) % exps), "exp", k) for k in range(1, exps)], axis=0
    ).reshape(-1, model_width)
    own_hidden = hidden_units(own_rows, in_weight[0, 0], inverse_gain)
    other_hidden = hidden_units(other_rows, in_weight[0, 0], inverse_gain, own_hidden)
    other_parts = down_part(other_hidden, down_weight[0, 0], jnp.bfloat16)
    other_parts = other_parts.reshape(exps - 1, contexts, capacity, model_width)
    own_part = down_part(own_hidden, down_weight[0, 0], jnp.float32)
    own_part = own_part.reshape(contexts, capacity, model_width)
    sums = [0.0] * per_context
    for k in range(exps):
        back = shift(other_parts[k - 1], "exp", -k).astype(jnp.float32) if k else own_part
        if per_context == 1:
            sums[0] = sums[0] + back
        else:
            place = (my_exp + k) % exps // group_size
            sums = [s + jnp.where(place == i, back, 0.0) for i, s in enumerate(sums)]
    weights = arrived_weights.reshape(contexts, per_context, capacity, 1)
    finished = arrived.astype(jnp.float32) * inverse_gain[0] + weights * jnp.stack(sums, axis=1)
    finished = finished.astype(jnp.bfloat16)

    def to_next_owner(rows, k):
        pipes = lax.axis_size("pipe")
        pairs = [
            (p * contexts + c, (p + 1) % pipes * contexts + (c - k) % contexts)
            for p in range(pipes)
            for c in range(contexts)
        ]
        return lax.ppermute(rows, ("pipe", "ctx"), pairs)

    returned = jnp.concatenate(
        [to_next_owner(finished[k], k).reshape(-1, model_width) for k in range(contexts)], axis=0
    )
    next_match = slot_ids[None, :] == next_slots[0].astype(jnp.int32)[:, None]
    layer = jnp.dot(next_match.astype(jnp.bfloat16), returned, preferred_element_type=jnp.float32)
    return layer.astype(jnp.bfloat16).reshape(1, 1, token_rows, model_width)


def solution(mesh):
    placed = (
        P("pipe", "exp", "ctx", None),
        P("pipe", "exp", "ctx", None),
        P("pipe", "exp", "ctx", None),
        P("pipe", "ctx", "exp"),
        P("pipe", None),
        P("pipe", ("ctx", "exp"), None, None),
        P("pipe", ("ctx", "exp"), None, None),
        P("pipe", "exp", "ctx", None),
        P("pipe", "exp", "ctx", None),
    )
    return jax.shard_map(
        on_device,
        mesh=mesh,
        in_specs=placed,
        out_specs=P("pipe", "exp", "ctx", None),
        check_vma=False,
    )
```

```python
import math

import jax
import jax.numpy as jnp
from jax import lax
from jax.sharding import PartitionSpec as P

QUERY_HEADS = 32
KEY_VALUE_HEADS = 2
HEAD_SIZE = 128


def shift(value, axis, by):
    devices = lax.axis_size(axis)
    return lax.ppermute(value, axis, [(i, (i + by) % devices) for i in range(devices)])


def after(value, *earlier):
    return lax.optimization_barrier((value, *earlier))[0]


def attend_block(query_block, key_rows, value_rows, row_ids, col_ids):
    scores = jnp.einsum(
        "qhd,kd->hqk", query_block, key_rows, preferred_element_type=jnp.float32
    ) * (1.0 / math.sqrt(HEAD_SIZE))
    scores = jnp.where((col_ids[None, :] <= row_ids[:, None])[None, :, :], scores, -jnp.inf)
    attention_weights = jax.nn.softmax(scores, axis=-1).astype(jnp.bfloat16)
    attended = jnp.einsum(
        "hqk,kd->qhd", attention_weights, value_rows, preferred_element_type=jnp.float32
    )
    return attended.astype(jnp.bfloat16)


def mixed_halves(queries, keys_values, residual, out_weight):
    contexts, exps = lax.axis_size("ctx"), lax.axis_size("exp")
    me, my_exp = lax.axis_index("ctx"), lax.axis_index("exp")
    rows = queries.shape[0]
    width = residual.shape[1]
    local_heads = QUERY_HEADS // contexts
    group_width = local_heads * HEAD_SIZE

    def pair_for(owner):
        head = owner * local_heads // (QUERY_HEADS // KEY_VALUE_HEADS)
        key = lax.dynamic_slice_in_dim(keys_values, head * HEAD_SIZE, HEAD_SIZE, 1)
        value = lax.dynamic_slice_in_dim(
            keys_values, (KEY_VALUE_HEADS + head) * HEAD_SIZE, HEAD_SIZE, 1
        )
        return jnp.concatenate([key, value], axis=1)

    def queries_for(owner):
        return lax.dynamic_slice_in_dim(queries, owner * group_width, group_width, 1)

    pairs = [pair_for(me)]
    blocks = [queries_for(me)]
    for k in range(1, contexts):
        pairs.append(shift(pair_for((me + k) % contexts), "ctx", k))
    for k in range(1, contexts):
        outgoing = queries_for((me + k) % contexts)
        if k > 1:
            outgoing = after(outgoing, blocks[1])
        blocks.append(shift(outgoing, "ctx", k))
    if exps == 2:
        weights = [out_weight, shift(out_weight, "exp", 1)]
        first = my_exp * (width // 2)
    else:
        gathered = lax.all_gather(out_weight, "exp", axis=1, tiled=True)
        weights = [gathered[:, : width // 2], gathered[:, width // 2 :]]
        first = 0
    offsets = [first, width // 2 - first]

    pair_rows = jnp.concatenate(pairs, axis=0)
    key_rows, value_rows = pair_rows[:, :HEAD_SIZE], pair_rows[:, HEAD_SIZE:]
    within = jnp.arange(rows, dtype=jnp.int32)
    origins = [(me - k) % contexts * rows for k in range(contexts)]
    col_ids = jnp.concatenate([origin + within for origin in origins])

    held, sent = [None, None], []
    for k in [*range(1, contexts), 0]:
        block = blocks[k] if k == 1 else after(blocks[k], *sent)
        attended = attend_block(
            block.reshape(rows, local_heads, HEAD_SIZE),
            key_rows,
            value_rows,
            origins[k] + within,
            col_ids,
        ).reshape(rows, group_width)
        terms, sent = [], []
        for half in range(2):
            term = jnp.dot(attended, weights[half], preferred_element_type=jnp.float32)
            if k == 0:
                own = lax.dynamic_slice_in_dim(residual, offsets[half], width // 2, 1)
                term = term + own.astype(jnp.float32)
            terms.append(lax.optimization_barrier(term))
        for half in range(2):
            term = terms[half]
            if held[half] is not None:
                term = term + held[half].astype(jnp.float32)
            if k == 0:
                held[half] = term
            else:
                sent.append(term.astype(jnp.bfloat16))
                held[half] = shift(sent[half], "ctx", 1)
    return held, first


def on_device(
    queries,
    rotated_keys_values,
    residual,
    out_weight,
    norm_gain,
    in_weight,
    down_weight,
    routes,
    route_weight,
):
    contexts, exps = lax.axis_size("ctx"), lax.axis_size("exp")
    me, my_exp = lax.axis_index("ctx"), lax.axis_index("exp")
    token_rows = queries.shape[2]
    model_width = residual.shape[3]
    group_size = min(4, exps)
    per_context = exps // group_size
    experts = contexts * per_context
    capacity = min(
        token_rows,
        group_size
        * ((3 * token_rows + 2 * experts * group_size - 1) // (2 * experts * group_size)),
    )
    slots = experts * capacity
    expert_ids = routes[0, 0, :, 0]
    expert_hits = (expert_ids[:, None] == jnp.arange(experts, dtype=jnp.int32)[None, :]).astype(
        jnp.int32
    )
    position = jnp.sum((jnp.cumsum(expert_hits, axis=0) - 1) * expert_hits, axis=1)
    distance = (expert_ids // per_context - me) % contexts
    slot_index = (distance * per_context + expert_ids % per_context) * capacity + position
    slot_ids = jnp.arange(slots, dtype=jnp.int32)
    slot_match = (slot_ids[:, None] == slot_index[None, :]).astype(jnp.bfloat16)
    hits = slot_ids[:, None] == slot_index[None, :]
    slot_weights = jnp.sum(jnp.where(hits, route_weight[0, 0, :, 0], 0.0), axis=1)
    told = jnp.concatenate([slot_weights, slot_index.astype(jnp.float32)])
    told = lax.all_gather(told, ("pipe", "ctx"))
    pipes, my_pipe = lax.axis_size("pipe"), lax.axis_index("pipe")
    width = per_context * capacity
    arrived_weights = [
        lax.dynamic_slice(told, (my_pipe * contexts + (me - k) % contexts, k * width), (1, width))
        for k in range(contexts)
    ]
    next_slots = lax.dynamic_slice(
        told, ((my_pipe - 1) % pipes * contexts + me, slots), (1, token_rows)
    )[0].astype(jnp.int32)

    halves, first = mixed_halves(
        queries[0, 0], rotated_keys_values[0, 0], residual[0, 0], out_weight[0]
    )
    mixed_rows = jnp.concatenate(halves, axis=1)
    if exps == 2:
        mixed_rows = jnp.where(first == 0, mixed_rows, jnp.concatenate(halves[::-1], axis=1))

    gain, inverse_gain = norm_gain[0], 1.0 / norm_gain[0]
    beside = next_slots[0].astype(jnp.float32) + sum(w[0, 0] for w in arrived_weights)
    scaled = (mixed_rows * (gain + beside * 0.0)).astype(jnp.bfloat16)
    packed = jnp.dot(slot_match, scaled, preferred_element_type=jnp.float32).astype(jnp.bfloat16)
    packed = packed.reshape(contexts, per_context, capacity, model_width)
    arrived = jnp.stack(
        [packed[0]] + [shift(packed[k], "ctx", k) for k in range(1, contexts)], axis=0
    )
    arrived = lax.optimization_barrier(arrived)

    def wanted_by(blocks, exp):
        if per_context == 1:
            return blocks[:, 0]
        return lax.dynamic_index_in_dim(blocks, exp // group_size, 1, keepdims=False)

    hidden_width = down_weight.shape[2]

    def expert_part(rows):
        rows = rows.reshape(-1, model_width)
        unscaled = rows.astype(jnp.float32) * inverse_gain
        mean_square = jnp.mean(unscaled * unscaled, axis=-1, keepdims=True)
        gate_up = jnp.dot(rows, in_weight[0, 0], preferred_element_type=jnp.float32)
        gate_up = gate_up * lax.rsqrt(mean_square + 1e-06)
        hidden = (jax.nn.silu(gate_up[:, :hidden_width]) * gate_up[:, hidden_width:]).astype(
            jnp.bfloat16
        )
        return jnp.dot(hidden, down_weight[0, 0], preferred_element_type=jnp.float32)

    others = [
        shift(wanted_by(arrived, (my_exp + k) % exps), "exp", k) for k in range(1, exps)
    ]
    own_part = lax.optimization_barrier(expert_part(wanted_by(arrived, my_exp)))
    own_part = own_part.reshape(contexts, capacity, model_width)
    other_parts = expert_part(jnp.concatenate(others, axis=0)).astype(jnp.bfloat16)
    other_parts = other_parts.reshape(exps - 1, contexts, capacity, model_width)
    sums = [0.0] * per_context
    for k in range(exps):
        back = shift(other_parts[k - 1], "exp", -k).astype(jnp.float32) if k else own_part
        if per_context == 1:
            sums[0] = sums[0] + back
        else:
            place = (my_exp + k) % exps // group_size
            sums = [s + jnp.where(place == i, back, 0.0) for i, s in enumerate(sums)]
    weights = jnp.stack(arrived_weights, axis=0).reshape(contexts, per_context, capacity, 1)
    finished = arrived.astype(jnp.float32) * inverse_gain + weights * jnp.stack(sums, axis=1)
    finished = finished.astype(jnp.bfloat16)

    def to_next_owner(rows, k):
        pipes = lax.axis_size("pipe")
        pairs = [
            (p * contexts + c, (p + 1) % pipes * contexts + (c - k) % contexts)
            for p in range(pipes)
            for c in range(contexts)
        ]
        return lax.ppermute(rows, ("pipe", "ctx"), pairs)

    returned = jnp.concatenate(
        [to_next_owner(finished[k], k).reshape(-1, model_width) for k in range(contexts)], axis=0
    )
    next_match = (slot_ids[None, :] == next_slots[:, None]).astype(jnp.bfloat16)
    layer = jnp.dot(next_match, returned, preferred_element_type=jnp.float32)
    return layer.astype(jnp.bfloat16).reshape(1, 1, token_rows, model_width)


def solution(mesh):
    placed = (
        P("pipe", "exp", "ctx", None),
        P("pipe", "exp", "ctx", None),
        P("pipe", "exp", "ctx", None),
        P("pipe", "ctx", "exp"),
        P("pipe", None),
        P("pipe", ("ctx", "exp"), None, None),
        P("pipe", ("ctx", "exp"), None, None),
        P("pipe", "exp", "ctx", None),
        P("pipe", "exp", "ctx", None),
    )
    return jax.shard_map(
        on_device,
        mesh=mesh,
        in_specs=placed,
        out_specs=P("pipe", "exp", "ctx", None),
        check_vma=False,
    )
```

```python
import math

import jax
import jax.numpy as jnp
from jax import lax
from jax.sharding import PartitionSpec as P

QUERY_HEADS = 32
KEY_VALUE_HEADS = 2
HEAD_SIZE = 128


def shift(value, axis, by):
    devices = lax.axis_size(axis)
    return lax.ppermute(value, axis, [(i, (i + by) % devices) for i in range(devices)])


def after(value, *earlier):
    return lax.optimization_barrier((value, *earlier))[0]


def attend_block(query_block, key_rows, value_rows, row_ids, col_ids):
    scores = jnp.einsum(
        "qhd,kd->hqk", query_block, key_rows, preferred_element_type=jnp.float32
    ) * (1.0 / math.sqrt(HEAD_SIZE))
    scores = jnp.where((col_ids[None, :] <= row_ids[:, None])[None, :, :], scores, -jnp.inf)
    attention_weights = jax.nn.softmax(scores, axis=-1).astype(jnp.bfloat16)
    attended = jnp.einsum(
        "hqk,kd->qhd", attention_weights, value_rows, preferred_element_type=jnp.float32
    )
    return attended.astype(jnp.bfloat16)


def mixed_halves(queries, keys_values, residual, out_weight):
    contexts, exps = lax.axis_size("ctx"), lax.axis_size("exp")
    me, my_exp = lax.axis_index("ctx"), lax.axis_index("exp")
    rows = queries.shape[0]
    width = residual.shape[1]
    local_heads = QUERY_HEADS // contexts
    group_width = local_heads * HEAD_SIZE

    def pair_for(owner):
        head = owner * local_heads // (QUERY_HEADS // KEY_VALUE_HEADS)
        key = lax.dynamic_slice_in_dim(keys_values, head * HEAD_SIZE, HEAD_SIZE, 1)
        value = lax.dynamic_slice_in_dim(
            keys_values, (KEY_VALUE_HEADS + head) * HEAD_SIZE, HEAD_SIZE, 1
        )
        return jnp.concatenate([key, value], axis=1)

    def queries_for(owner):
        return lax.dynamic_slice_in_dim(queries, owner * group_width, group_width, 1)

    pairs = [pair_for(me)]
    blocks = [queries_for(me)]
    for k in range(1, contexts):
        pairs.append(shift(pair_for((me + k) % contexts), "ctx", k))
    for k in range(1, contexts):
        outgoing = queries_for((me + k) % contexts)
        if k > 1:
            outgoing = after(outgoing, blocks[1])
        blocks.append(shift(outgoing, "ctx", k))
    if exps == 2:
        weights = [out_weight, shift(out_weight, "exp", 1)]
        first = my_exp * (width // 2)
    else:
        gathered = lax.all_gather(out_weight, "exp", axis=1, tiled=True)
        weights = [gathered[:, : width // 2], gathered[:, width // 2 :]]
        first = 0
    offsets = [first, width // 2 - first]

    pair_rows = jnp.concatenate(pairs, axis=0)
    key_rows, value_rows = pair_rows[:, :HEAD_SIZE], pair_rows[:, HEAD_SIZE:]
    within = jnp.arange(rows, dtype=jnp.int32)
    origins = [(me - k) % contexts * rows for k in range(contexts)]
    col_ids = jnp.concatenate([origin + within for origin in origins])

    held, sent = [None, None], []
    for k in [*range(1, contexts), 0]:
        block = blocks[k] if k == 1 else after(blocks[k], *sent)
        attended = attend_block(
            block.reshape(rows, local_heads, HEAD_SIZE),
            key_rows,
            value_rows,
            origins[k] + within,
            col_ids,
        ).reshape(rows, group_width)
        terms, sent = [], []
        for half in range(2):
            term = jnp.dot(attended, weights[half], preferred_element_type=jnp.float32)
            if k == 0:
                own = lax.dynamic_slice_in_dim(residual, offsets[half], width // 2, 1)
                term = term + own.astype(jnp.float32)
            terms.append(lax.optimization_barrier(term))
        for half in range(2):
            term = terms[half]
            if held[half] is not None:
                term = term + held[half].astype(jnp.float32)
            if k == 0:
                held[half] = term
            else:
                sent.append(term.astype(jnp.bfloat16))
                held[half] = shift(sent[half], "ctx", 1)
    return held, first


def on_device(
    queries,
    rotated_keys_values,
    residual,
    out_weight,
    norm_gain,
    in_weight,
    down_weight,
    routes,
    route_weight,
):
    contexts, exps = lax.axis_size("ctx"), lax.axis_size("exp")
    me, my_exp = lax.axis_index("ctx"), lax.axis_index("exp")
    token_rows = queries.shape[2]
    model_width = residual.shape[3]
    group_size = min(4, exps)
    per_context = exps // group_size
    experts = contexts * per_context
    capacity = min(
        token_rows,
        group_size
        * ((3 * token_rows + 2 * experts * group_size - 1) // (2 * experts * group_size)),
    )
    slots = experts * capacity
    expert_ids = routes[0, 0, :, 0]
    expert_hits = (expert_ids[:, None] == jnp.arange(experts, dtype=jnp.int32)[None, :]).astype(
        jnp.int32
    )
    position = jnp.sum((jnp.cumsum(expert_hits, axis=0) - 1) * expert_hits, axis=1)
    distance = (expert_ids // per_context - me) % contexts
    slot_index = (distance * per_context + expert_ids % per_context) * capacity + position
    slot_ids = jnp.arange(slots, dtype=jnp.int32)
    slot_match = (slot_ids[:, None] == slot_index[None, :]).astype(jnp.bfloat16)
    halves, first = mixed_halves(
        queries[0, 0], rotated_keys_values[0, 0], residual[0, 0], out_weight[0]
    )
    mixed_rows = jnp.concatenate(halves, axis=1)
    if exps == 2:
        mixed_rows = jnp.where(first == 0, mixed_rows, jnp.concatenate(halves[::-1], axis=1))

    gain, inverse_gain = norm_gain[0], 1.0 / norm_gain[0]
    weights = route_weight[0, 0]
    coarse = lax.reduce_precision(weights, exponent_bits=8, mantissa_bits=7)
    beside = jnp.pad(jnp.concatenate([coarse, weights - coarse], axis=1), ((0, 0), (0, 126)))
    scaled = jnp.concatenate([mixed_rows * gain, beside], axis=1).astype(jnp.bfloat16)
    packed = jnp.dot(slot_match, scaled, preferred_element_type=jnp.float32).astype(jnp.bfloat16)
    packed = packed.reshape(contexts, per_context, capacity, model_width + 128)
    blocks = [packed[0]] + [shift(packed[k], "ctx", k) for k in range(1, contexts)]
    arrived = jnp.stack([block[..., :model_width] for block in blocks], axis=0)
    weights = jnp.stack([block[..., model_width:] for block in blocks], axis=0)
    weights = weights[..., 0:1].astype(jnp.float32) + weights[..., 1:2].astype(jnp.float32)
    arrived = lax.optimization_barrier(arrived)

    def wanted_by(blocks, exp):
        if per_context == 1:
            return blocks[:, 0]
        return lax.dynamic_index_in_dim(blocks, exp // group_size, 1, keepdims=False)

    hidden_width = down_weight.shape[2]

    def expert_part(rows):
        rows = lax.optimization_barrier(rows.reshape(-1, model_width))
        unscaled = rows.astype(jnp.float32) * inverse_gain
        mean_square = jnp.mean(unscaled * unscaled, axis=-1, keepdims=True)
        gate_up = jnp.dot(rows, in_weight[0, 0], preferred_element_type=jnp.float32)
        gate_up = gate_up * lax.rsqrt(mean_square + 1e-06)
        hidden = (jax.nn.silu(gate_up[:, :hidden_width]) * gate_up[:, hidden_width:]).astype(
            jnp.bfloat16
        )
        return jnp.dot(hidden, down_weight[0, 0], preferred_element_type=jnp.float32)

    others = [
        shift(wanted_by(arrived, (my_exp + k) % exps), "exp", k) for k in range(1, exps)
    ]
    own_part = lax.optimization_barrier(expert_part(wanted_by(arrived, my_exp)))
    own_part = own_part.reshape(contexts, capacity, model_width)
    other_parts = expert_part(jnp.concatenate(others, axis=0)).astype(jnp.bfloat16)
    other_parts = other_parts.reshape(exps - 1, contexts, capacity, model_width)
    sums = [0.0] * per_context
    for k in range(exps):
        back = shift(other_parts[k - 1], "exp", -k).astype(jnp.float32) if k else own_part
        if per_context == 1:
            sums[0] = sums[0] + back
        else:
            place = (my_exp + k) % exps // group_size
            sums = [s + jnp.where(place == i, back, 0.0) for i, s in enumerate(sums)]
    finished = arrived.astype(jnp.float32) * inverse_gain + weights * jnp.stack(sums, axis=1)
    finished = finished.astype(jnp.bfloat16)

    def to_next_owner(rows, k):
        pipes = lax.axis_size("pipe")
        pairs = [
            (p * contexts + c, (p + 1) % pipes * contexts + (c - k) % contexts)
            for p in range(pipes)
            for c in range(contexts)
        ]
        return lax.ppermute(rows, ("pipe", "ctx"), pairs)

    returned = [to_next_owner(finished[k], k).reshape(-1, model_width) for k in range(contexts)]
    next_slots = slot_index.astype(jnp.float32) + returned[0][0, 0].astype(jnp.float32) * 0.0
    next_slots = shift(next_slots[None, :], "pipe", 1)[0].astype(jnp.int32)
    next_match = (slot_ids[None, :] == next_slots[:, None]).astype(jnp.bfloat16)
    returned = jnp.concatenate(returned, axis=0)
    layer = jnp.dot(next_match, returned, preferred_element_type=jnp.float32)
    return layer.astype(jnp.bfloat16).reshape(1, 1, token_rows, model_width)


def solution(mesh):
    placed = (
        P("pipe", "exp", "ctx", None),
        P("pipe", "exp", "ctx", None),
        P("pipe", "exp", "ctx", None),
        P("pipe", "ctx", "exp"),
        P("pipe", None),
        P("pipe", ("ctx", "exp"), None, None),
        P("pipe", ("ctx", "exp"), None, None),
        P("pipe", "exp", "ctx", None),
        P("pipe", "exp", "ctx", None),
    )
    return jax.shard_map(
        on_device,
        mesh=mesh,
        in_specs=placed,
        out_specs=P("pipe", "exp", "ctx", None),
        check_vma=False,
    )
```

```python
import math

import jax
import jax.numpy as jnp
from jax import lax
from jax.sharding import PartitionSpec as P

QUERY_HEADS = 32
KEY_VALUE_HEADS = 2
HEAD_SIZE = 128


def shift(value, axis, by):
    devices = lax.axis_size(axis)
    return lax.ppermute(value, axis, [(i, (i + by) % devices) for i in range(devices)])


def after(value, *earlier):
    return lax.optimization_barrier((value, *earlier))[0]


def attend_block(query_block, key_rows, value_rows, row_ids, col_ids):
    scores = jnp.einsum(
        "qhd,kd->hqk", query_block, key_rows, preferred_element_type=jnp.float32
    ) * (1.0 / math.sqrt(HEAD_SIZE))
    scores = jnp.where((col_ids[None, :] <= row_ids[:, None])[None, :, :], scores, -jnp.inf)
    attention_weights = jax.nn.softmax(scores, axis=-1).astype(jnp.bfloat16)
    attended = jnp.einsum(
        "hqk,kd->qhd", attention_weights, value_rows, preferred_element_type=jnp.float32
    )
    return attended.astype(jnp.bfloat16)


def mixed_halves(queries, keys_values, residual, out_weight, slots_here):
    contexts, exps = lax.axis_size("ctx"), lax.axis_size("exp")
    me, my_exp = lax.axis_index("ctx"), lax.axis_index("exp")
    rows = queries.shape[0]
    width = residual.shape[1]
    local_heads = QUERY_HEADS // contexts
    group_width = local_heads * HEAD_SIZE

    def pair_for(owner):
        head = owner * local_heads // (QUERY_HEADS // KEY_VALUE_HEADS)
        key = lax.dynamic_slice_in_dim(keys_values, head * HEAD_SIZE, HEAD_SIZE, 1)
        value = lax.dynamic_slice_in_dim(
            keys_values, (KEY_VALUE_HEADS + head) * HEAD_SIZE, HEAD_SIZE, 1
        )
        return jnp.concatenate([key, value], axis=1)

    def queries_for(owner):
        return lax.dynamic_slice_in_dim(queries, owner * group_width, group_width, 1)

    pairs = [pair_for(me)]
    blocks = [queries_for(me)]
    for k in range(1, contexts):
        pairs.append(shift(pair_for((me + k) % contexts), "ctx", k))
    for k in range(1, contexts):
        outgoing = queries_for((me + k) % contexts)
        if k > 1:
            outgoing = after(outgoing, blocks[1])
        blocks.append(shift(outgoing, "ctx", k))
    if exps == 2:
        weights = [out_weight, shift(out_weight, "exp", 1)]
        first = my_exp * (width // 2)
    else:
        gathered = lax.all_gather(out_weight, "exp", axis=1, tiled=True)
        weights = [gathered[:, : width // 2], gathered[:, width // 2 :]]
        first = 0
    offsets = [first, width // 2 - first]

    pair_rows = jnp.concatenate(pairs, axis=0)
    key_rows, value_rows = pair_rows[:, :HEAD_SIZE], pair_rows[:, HEAD_SIZE:]
    within = jnp.arange(rows, dtype=jnp.int32)
    origins = [(me - k) % contexts * rows for k in range(contexts)]
    col_ids = jnp.concatenate([origin + within for origin in origins])

    held, sent, next_slots = [None, None], [], shift(slots_here, "pipe", 1)
    for k in [*range(1, contexts), 0]:
        behind = sum(block[0, 0] * 0.0 for block in sent)
        attended = attend_block(
            (blocks[k] + behind).reshape(rows, local_heads, HEAD_SIZE),
            key_rows,
            value_rows,
            origins[k] + within,
            col_ids,
        ).reshape(rows, group_width)
        sent = []
        terms = []
        for half in range(2):
            term = jnp.dot(attended, weights[half], preferred_element_type=jnp.float32)
            if k == 0:
                own = lax.dynamic_slice_in_dim(residual, offsets[half], width // 2, 1)
                term = term + own.astype(jnp.float32)
            if k == 1 and half == 0:
                term = term + weights[1][0, 0].astype(jnp.float32) * 0.0
            terms.append(lax.optimization_barrier(term))
        for half in range(2):
            term = terms[half]
            if held[half] is not None:
                term = term + held[half].astype(jnp.float32)
            if k == 0:
                held[half] = term + next_slots[0, 0] * 0.0
            else:
                sent.append(term.astype(jnp.bfloat16))
                held[half] = shift(sent[half], "ctx", 1)
    return held, first, next_slots[0].astype(jnp.int32)


def on_device(
    queries,
    rotated_keys_values,
    residual,
    out_weight,
    norm_gain,
    in_weight,
    down_weight,
    routes,
    route_weight,
):
    contexts, exps = lax.axis_size("ctx"), lax.axis_size("exp")
    me, my_exp = lax.axis_index("ctx"), lax.axis_index("exp")
    token_rows = queries.shape[2]
    model_width = residual.shape[3]
    group_size = min(4, exps)
    per_context = exps // group_size
    experts = contexts * per_context
    capacity = min(
        token_rows,
        group_size
        * ((3 * token_rows + 2 * experts * group_size - 1) // (2 * experts * group_size)),
    )
    slots = experts * capacity
    expert_ids = routes[0, 0, :, 0]
    expert_hits = (expert_ids[:, None] == jnp.arange(experts, dtype=jnp.int32)[None, :]).astype(
        jnp.int32
    )
    position = jnp.sum((jnp.cumsum(expert_hits, axis=0) - 1) * expert_hits, axis=1)
    distance = (expert_ids // per_context - me) % contexts
    slot_index = (distance * per_context + expert_ids % per_context) * capacity + position
    slot_ids = jnp.arange(slots, dtype=jnp.int32)
    slot_match = (slot_ids[:, None] == slot_index[None, :]).astype(jnp.bfloat16)
    halves, first, next_slots = mixed_halves(
        queries[0, 0],
        rotated_keys_values[0, 0],
        residual[0, 0],
        out_weight[0],
        slot_index.astype(jnp.float32)[None, :],
    )
    mixed_rows = jnp.concatenate(halves, axis=1)
    if exps == 2:
        mixed_rows = jnp.where(first == 0, mixed_rows, jnp.concatenate(halves[::-1], axis=1))

    gain, inverse_gain = norm_gain[0], 1.0 / norm_gain[0]
    weights = route_weight[0, 0]
    coarse = lax.reduce_precision(weights, exponent_bits=8, mantissa_bits=7)
    beside = jnp.pad(jnp.concatenate([coarse, weights - coarse], axis=1), ((0, 0), (0, 126)))
    scaled = jnp.concatenate([mixed_rows * gain, beside], axis=1).astype(jnp.bfloat16)
    packed = jnp.dot(slot_match, scaled, preferred_element_type=jnp.float32).astype(jnp.bfloat16)
    packed = packed.reshape(contexts, per_context, capacity, model_width + 128)
    blocks = [packed[0]] + [shift(packed[k], "ctx", k) for k in range(1, contexts)]
    arrived = jnp.stack([block[..., :model_width] for block in blocks], axis=0)
    weights = jnp.stack([block[..., model_width:] for block in blocks], axis=0)
    weights = weights[..., 0:1].astype(jnp.float32) + weights[..., 1:2].astype(jnp.float32)
    arrived = lax.optimization_barrier(arrived)

    def wanted_by(blocks, exp):
        if per_context == 1:
            return blocks[:, 0]
        return lax.dynamic_index_in_dim(blocks, exp // group_size, 1, keepdims=False)

    hidden_width = down_weight.shape[2]

    def gate_and_up(rows, behind):
        rows = lax.optimization_barrier(rows.reshape(-1, model_width))
        unscaled = rows.astype(jnp.float32) * inverse_gain + behind
        mean_square = jnp.mean(unscaled * unscaled, axis=-1, keepdims=True)
        gate_up = jnp.dot(rows, in_weight[0, 0], preferred_element_type=jnp.float32)
        return gate_up * lax.rsqrt(mean_square + 1e-06)

    def down_part(gate_up):
        hidden = (jax.nn.silu(gate_up[:, :hidden_width]) * gate_up[:, hidden_width:]).astype(
            jnp.bfloat16
        )
        return jnp.dot(hidden, down_weight[0, 0], preferred_element_type=jnp.float32)

    others = [
        shift(wanted_by(arrived, (my_exp + k) % exps), "exp", k) for k in range(1, exps)
    ]
    own_gate_up = lax.optimization_barrier(gate_and_up(wanted_by(arrived, my_exp), 0.0))
    other_gate_up = gate_and_up(jnp.concatenate(others, axis=0), own_gate_up[0, 0] * 0.0)
    other_parts = down_part(other_gate_up).astype(jnp.bfloat16)
    own_part = lax.optimization_barrier(down_part(own_gate_up))
    own_part = own_part.reshape(contexts, capacity, model_width)
    other_parts = other_parts.reshape(exps - 1, contexts, capacity, model_width)
    sums = [0.0] * per_context
    for k in range(exps):
        back = shift(other_parts[k - 1], "exp", -k).astype(jnp.float32) if k else own_part
        if per_context == 1:
            sums[0] = sums[0] + back
        else:
            place = (my_exp + k) % exps // group_size
            sums = [s + jnp.where(place == i, back, 0.0) for i, s in enumerate(sums)]
    finished = arrived.astype(jnp.float32) * inverse_gain + weights * jnp.stack(sums, axis=1)
    finished = finished.astype(jnp.bfloat16)

    def to_next_owner(rows, k):
        pipes = lax.axis_size("pipe")
        pairs = [
            (p * contexts + c, (p + 1) % pipes * contexts + (c - k) % contexts)
            for p in range(pipes)
            for c in range(contexts)
        ]
        return lax.ppermute(rows, ("pipe", "ctx"), pairs)

    returned = [to_next_owner(finished[k], k).reshape(-1, model_width) for k in range(contexts)]
    next_match = (slot_ids[None, :] == next_slots[:, None]).astype(jnp.bfloat16)
    returned = jnp.concatenate(returned, axis=0)
    layer = jnp.dot(next_match, returned, preferred_element_type=jnp.float32)
    return layer.astype(jnp.bfloat16).reshape(1, 1, token_rows, model_width)


def solution(mesh):
    placed = (
        P("pipe", "exp", "ctx", None),
        P("pipe", "exp", "ctx", None),
        P("pipe", "exp", "ctx", None),
        P("pipe", "ctx", "exp"),
        P("pipe", None),
        P("pipe", ("ctx", "exp"), None, None),
        P("pipe", ("ctx", "exp"), None, None),
        P("pipe", "exp", "ctx", None),
        P("pipe", "exp", "ctx", None),
    )
    return jax.shard_map(
        on_device,
        mesh=mesh,
        in_specs=placed,
        out_specs=P("pipe", "exp", "ctx", None),
        check_vma=False,
    )
```

```python
import math

import jax
import jax.numpy as jnp
from jax import lax
from jax.sharding import PartitionSpec as P

QUERY_HEADS = 32
KEY_VALUE_HEADS = 2
HEAD_SIZE = 128


def shift(value, axis, by):
    devices = lax.axis_size(axis)
    return lax.ppermute(value, axis, [(i, (i + by) % devices) for i in range(devices)])


def after(value, *earlier):
    return lax.optimization_barrier((value, *earlier))[0]


def attend_block(query_block, key_rows, value_rows, row_ids, col_ids):
    scores = jnp.einsum(
        "qhd,kd->hqk", query_block, key_rows, preferred_element_type=jnp.float32
    ) * (1.0 / math.sqrt(HEAD_SIZE))
    scores = jnp.where((col_ids[None, :] <= row_ids[:, None])[None, :, :], scores, -jnp.inf)
    attention_weights = jax.nn.softmax(scores, axis=-1).astype(jnp.bfloat16)
    attended = jnp.einsum(
        "hqk,kd->qhd", attention_weights, value_rows, preferred_element_type=jnp.float32
    )
    return attended.astype(jnp.bfloat16)


def mixed_halves(queries, keys_values, residual, out_weight, slots_here):
    contexts, exps = lax.axis_size("ctx"), lax.axis_size("exp")
    me, my_exp = lax.axis_index("ctx"), lax.axis_index("exp")
    rows = queries.shape[0]
    width = residual.shape[1]
    local_heads = QUERY_HEADS // contexts
    group_width = local_heads * HEAD_SIZE

    def pair_for(owner):
        head = owner * local_heads // (QUERY_HEADS // KEY_VALUE_HEADS)
        key = lax.dynamic_slice_in_dim(keys_values, head * HEAD_SIZE, HEAD_SIZE, 1)
        value = lax.dynamic_slice_in_dim(
            keys_values, (KEY_VALUE_HEADS + head) * HEAD_SIZE, HEAD_SIZE, 1
        )
        return jnp.concatenate([key, value], axis=1)

    def queries_for(owner):
        return lax.dynamic_slice_in_dim(queries, owner * group_width, group_width, 1)

    pairs = [pair_for(me)]
    blocks = [queries_for(me)]
    for k in range(1, contexts):
        pairs.append(shift(pair_for((me + k) % contexts), "ctx", k))
    for k in range(1, contexts):
        outgoing = queries_for((me + k) % contexts)
        if k > 1:
            outgoing = after(outgoing, blocks[1])
        blocks.append(shift(outgoing, "ctx", k))
    if exps == 2:
        weights = [out_weight, shift(out_weight, "exp", 1)]
        first = my_exp * (width // 2)
    else:
        gathered = lax.all_gather(out_weight, "exp", axis=1, tiled=True)
        weights = [gathered[:, : width // 2], gathered[:, width // 2 :]]
        first = 0
    offsets = [first, width // 2 - first]

    pair_rows = jnp.concatenate(pairs, axis=0)
    key_rows, value_rows = pair_rows[:, :HEAD_SIZE], pair_rows[:, HEAD_SIZE:]
    within = jnp.arange(rows, dtype=jnp.int32)
    origins = [(me - k) % contexts * rows for k in range(contexts)]
    col_ids = jnp.concatenate([origin + within for origin in origins])

    held, sent, next_slots = [None, None], [], None
    for k in [*range(1, contexts), 0]:
        behind = sum(block[0, 0] * 0.0 for block in sent)
        attended = attend_block(
            (blocks[k] + behind).reshape(rows, local_heads, HEAD_SIZE),
            key_rows,
            value_rows,
            origins[k] + within,
            col_ids,
        ).reshape(rows, group_width)
        if k == contexts - 1:
            next_slots = shift(slots_here + behind, "pipe", 1)
        sent = []
        terms = []
        for half in range(2):
            term = jnp.dot(attended, weights[half], preferred_element_type=jnp.float32)
            if k == 0:
                own = lax.dynamic_slice_in_dim(residual, offsets[half], width // 2, 1)
                term = term + own.astype(jnp.float32)
            if k == 1 and half == 0:
                term = term + weights[1][0, 0].astype(jnp.float32) * 0.0
            terms.append(lax.optimization_barrier(term))
        for half in range(2):
            term = terms[half]
            if held[half] is not None:
                term = term + held[half].astype(jnp.float32)
            if k == 0:
                held[half] = term + next_slots[0, 0] * 0.0
            else:
                sent.append(term.astype(jnp.bfloat16))
                held[half] = shift(sent[half], "ctx", 1)
    return held, first, next_slots[0].astype(jnp.int32)


def on_device(
    queries,
    rotated_keys_values,
    residual,
    out_weight,
    norm_gain,
    in_weight,
    down_weight,
    routes,
    route_weight,
):
    contexts, exps = lax.axis_size("ctx"), lax.axis_size("exp")
    me, my_exp = lax.axis_index("ctx"), lax.axis_index("exp")
    token_rows = queries.shape[2]
    model_width = residual.shape[3]
    group_size = min(4, exps)
    per_context = exps // group_size
    experts = contexts * per_context
    capacity = min(
        token_rows,
        group_size
        * ((3 * token_rows + 2 * experts * group_size - 1) // (2 * experts * group_size)),
    )
    slots = experts * capacity
    expert_ids = routes[0, 0, :, 0]
    expert_hits = (expert_ids[:, None] == jnp.arange(experts, dtype=jnp.int32)[None, :]).astype(
        jnp.int32
    )
    position = jnp.sum((jnp.cumsum(expert_hits, axis=0) - 1) * expert_hits, axis=1)
    distance = (expert_ids // per_context - me) % contexts
    slot_index = (distance * per_context + expert_ids % per_context) * capacity + position
    slot_ids = jnp.arange(slots, dtype=jnp.int32)
    slot_match = (slot_ids[:, None] == slot_index[None, :]).astype(jnp.bfloat16)
    halves, first, next_slots = mixed_halves(
        queries[0, 0],
        rotated_keys_values[0, 0],
        residual[0, 0],
        out_weight[0],
        slot_index.astype(jnp.float32)[None, :],
    )
    mixed_rows = jnp.concatenate(halves, axis=1)
    if exps == 2:
        mixed_rows = jnp.where(first == 0, mixed_rows, jnp.concatenate(halves[::-1], axis=1))

    gain, inverse_gain = norm_gain[0], 1.0 / norm_gain[0]
    weights = route_weight[0, 0]
    coarse = lax.reduce_precision(weights, exponent_bits=8, mantissa_bits=7)
    beside = jnp.pad(jnp.concatenate([coarse, weights - coarse], axis=1), ((0, 0), (0, 126)))
    scaled = jnp.concatenate([mixed_rows * gain, beside], axis=1).astype(jnp.bfloat16)
    packed = jnp.dot(slot_match, scaled, preferred_element_type=jnp.float32).astype(jnp.bfloat16)
    packed = packed.reshape(contexts, per_context, capacity, model_width + 128)
    blocks = [packed[0]] + [shift(packed[k], "ctx", k) for k in range(1, contexts)]
    arrived = jnp.stack([block[..., :model_width] for block in blocks], axis=0)
    weights = jnp.stack([block[..., model_width:] for block in blocks], axis=0)
    weights = weights[..., 0:1].astype(jnp.float32) + weights[..., 1:2].astype(jnp.float32)
    arrived = lax.optimization_barrier(arrived)

    def wanted_by(blocks, exp):
        if per_context == 1:
            return blocks[:, 0]
        return lax.dynamic_index_in_dim(blocks, exp // group_size, 1, keepdims=False)

    hidden_width = down_weight.shape[2]

    def gate_and_up(rows, behind):
        rows = lax.optimization_barrier(rows.reshape(-1, model_width))
        unscaled = rows.astype(jnp.float32) * inverse_gain + behind
        mean_square = jnp.mean(unscaled * unscaled, axis=-1, keepdims=True)
        gate_up = jnp.dot(rows, in_weight[0, 0], preferred_element_type=jnp.float32)
        return gate_up * lax.rsqrt(mean_square + 1e-06)

    def down_part(gate_up):
        hidden = (jax.nn.silu(gate_up[:, :hidden_width]) * gate_up[:, hidden_width:]).astype(
            jnp.bfloat16
        )
        return jnp.dot(hidden, down_weight[0, 0], preferred_element_type=jnp.float32)

    others = [
        shift(wanted_by(arrived, (my_exp + k) % exps), "exp", k) for k in range(1, exps)
    ]
    own_gate_up = lax.optimization_barrier(gate_and_up(wanted_by(arrived, my_exp), 0.0))
    other_gate_up = gate_and_up(jnp.concatenate(others, axis=0), own_gate_up[0, 0] * 0.0)
    other_parts = down_part(other_gate_up).astype(jnp.bfloat16)
    own_part = lax.optimization_barrier(down_part(own_gate_up))
    own_part = own_part.reshape(contexts, capacity, model_width)
    other_parts = other_parts.reshape(exps - 1, contexts, capacity, model_width)
    sums = [0.0] * per_context
    for k in range(exps):
        back = shift(other_parts[k - 1], "exp", -k).astype(jnp.float32) if k else own_part
        if per_context == 1:
            sums[0] = sums[0] + back
        else:
            place = (my_exp + k) % exps // group_size
            sums = [s + jnp.where(place == i, back, 0.0) for i, s in enumerate(sums)]
    finished = arrived.astype(jnp.float32) * inverse_gain + weights * jnp.stack(sums, axis=1)
    finished = finished.astype(jnp.bfloat16)

    def to_next_owner(rows, k):
        pipes = lax.axis_size("pipe")
        pairs = [
            (p * contexts + c, (p + 1) % pipes * contexts + (c - k) % contexts)
            for p in range(pipes)
            for c in range(contexts)
        ]
        return lax.ppermute(rows, ("pipe", "ctx"), pairs)

    returned = [to_next_owner(finished[k], k).reshape(-1, model_width) for k in range(contexts)]
    next_match = (slot_ids[None, :] == next_slots[:, None]).astype(jnp.bfloat16)
    returned = jnp.concatenate(returned, axis=0)
    layer = jnp.dot(next_match, returned, preferred_element_type=jnp.float32)
    return layer.astype(jnp.bfloat16).reshape(1, 1, token_rows, model_width)


def solution(mesh):
    placed = (
        P("pipe", "exp", "ctx", None),
        P("pipe", "exp", "ctx", None),
        P("pipe", "exp", "ctx", None),
        P("pipe", "ctx", "exp"),
        P("pipe", None),
        P("pipe", ("ctx", "exp"), None, None),
        P("pipe", ("ctx", "exp"), None, None),
        P("pipe", "exp", "ctx", None),
        P("pipe", "exp", "ctx", None),
    )
    return jax.shard_map(
        on_device,
        mesh=mesh,
        in_specs=placed,
        out_specs=P("pipe", "exp", "ctx", None),
        check_vma=False,
    )
```

```python
import math

import jax
import jax.numpy as jnp
from jax import lax
from jax.sharding import PartitionSpec as P

QUERY_HEADS = 32
KEY_VALUE_HEADS = 2
HEAD_SIZE = 128


def shift(value, axis, by):
    devices = lax.axis_size(axis)
    return lax.ppermute(value, axis, [(i, (i + by) % devices) for i in range(devices)])


def after(value, *earlier):
    return lax.optimization_barrier((value, *earlier))[0]


def attend_block(query_block, key_rows, value_rows, row_ids, col_ids):
    scores = jnp.einsum(
        "qhd,kd->hqk", query_block, key_rows, preferred_element_type=jnp.float32
    ) * (1.0 / math.sqrt(HEAD_SIZE))
    scores = jnp.where((col_ids[None, :] <= row_ids[:, None])[None, :, :], scores, -jnp.inf)
    attention_weights = jax.nn.softmax(scores, axis=-1).astype(jnp.bfloat16)
    attended = jnp.einsum(
        "hqk,kd->qhd", attention_weights, value_rows, preferred_element_type=jnp.float32
    )
    return attended.astype(jnp.bfloat16)


def mixed_halves(queries, keys_values, residual, out_weight, slots_here):
    contexts, exps = lax.axis_size("ctx"), lax.axis_size("exp")
    me, my_exp = lax.axis_index("ctx"), lax.axis_index("exp")
    rows = queries.shape[0]
    width = residual.shape[1]
    local_heads = QUERY_HEADS // contexts
    group_width = local_heads * HEAD_SIZE

    def pair_for(owner):
        head = owner * local_heads // (QUERY_HEADS // KEY_VALUE_HEADS)
        key = lax.dynamic_slice_in_dim(keys_values, head * HEAD_SIZE, HEAD_SIZE, 1)
        value = lax.dynamic_slice_in_dim(
            keys_values, (KEY_VALUE_HEADS + head) * HEAD_SIZE, HEAD_SIZE, 1
        )
        return jnp.concatenate([key, value], axis=1)

    def queries_for(owner):
        return lax.dynamic_slice_in_dim(queries, owner * group_width, group_width, 1)

    pairs = [pair_for(me)]
    blocks = [queries_for(me)]
    for k in range(1, contexts):
        pairs.append(shift(pair_for((me + k) % contexts), "ctx", k))
    for k in range(1, contexts):
        outgoing = queries_for((me + k) % contexts)
        if k > 1:
            outgoing = after(outgoing, blocks[1])
        blocks.append(shift(outgoing, "ctx", k))
    if exps == 2:
        weights = [out_weight, shift(out_weight, "exp", 1)]
        first = my_exp * (width // 2)
    else:
        gathered = lax.all_gather(out_weight, "exp", axis=1, tiled=True)
        weights = [gathered[:, : width // 2], gathered[:, width // 2 :]]
        first = 0
    offsets = [first, width // 2 - first]

    pair_rows = jnp.concatenate(pairs, axis=0)
    key_rows, value_rows = pair_rows[:, :HEAD_SIZE], pair_rows[:, HEAD_SIZE:]
    within = jnp.arange(rows, dtype=jnp.int32)
    origins = [(me - k) % contexts * rows for k in range(contexts)]
    col_ids = jnp.concatenate([origin + within for origin in origins])

    held, sent, next_slots = [None, None], [], None
    for k in [*range(1, contexts), 0]:
        behind = sum(block[0, 0] * 0.0 for block in sent)
        attended = attend_block(
            (blocks[k] + behind).reshape(rows, local_heads, HEAD_SIZE),
            key_rows,
            value_rows,
            origins[k] + within,
            col_ids,
        ).reshape(rows, group_width)
        if k == contexts - 1:
            next_slots = shift(slots_here + behind, "pipe", 1)
        sent = []
        terms = []
        for half in range(2):
            term = jnp.dot(attended, weights[half], preferred_element_type=jnp.float32)
            if k == 0:
                own = lax.dynamic_slice_in_dim(residual, offsets[half], width // 2, 1)
                term = term + own.astype(jnp.float32)
            if k == 1 and half == 1 and contexts > 2:
                term = term + blocks[2][0, 0].astype(jnp.float32) * 0.0
            terms.append(lax.optimization_barrier(term))
        for half in range(2):
            term = terms[half]
            if held[half] is not None:
                term = term + held[half].astype(jnp.float32)
            if k == 0:
                held[half] = term + next_slots[0, 0] * 0.0
            else:
                sent.append(term.astype(jnp.bfloat16))
                held[half] = shift(sent[half], "ctx", 1)
    return held, first, next_slots[0].astype(jnp.int32)


def on_device(
    queries,
    rotated_keys_values,
    residual,
    out_weight,
    norm_gain,
    in_weight,
    down_weight,
    routes,
    route_weight,
):
    contexts, exps = lax.axis_size("ctx"), lax.axis_size("exp")
    me, my_exp = lax.axis_index("ctx"), lax.axis_index("exp")
    token_rows = queries.shape[2]
    model_width = residual.shape[3]
    group_size = min(4, exps)
    per_context = exps // group_size
    experts = contexts * per_context
    capacity = min(
        token_rows,
        group_size
        * ((3 * token_rows + 2 * experts * group_size - 1) // (2 * experts * group_size)),
    )
    slots = experts * capacity
    expert_ids = routes[0, 0, :, 0]
    expert_hits = (expert_ids[:, None] == jnp.arange(experts, dtype=jnp.int32)[None, :]).astype(
        jnp.int32
    )
    position = jnp.sum((jnp.cumsum(expert_hits, axis=0) - 1) * expert_hits, axis=1)
    distance = (expert_ids // per_context - me) % contexts
    slot_index = (distance * per_context + expert_ids % per_context) * capacity + position
    slot_ids = jnp.arange(slots, dtype=jnp.int32)
    slot_match = (slot_ids[:, None] == slot_index[None, :]).astype(jnp.bfloat16)
    halves, first, next_slots = mixed_halves(
        queries[0, 0],
        rotated_keys_values[0, 0],
        residual[0, 0],
        out_weight[0],
        slot_index.astype(jnp.float32)[None, :],
    )
    mixed_rows = jnp.concatenate(halves, axis=1)
    if exps == 2:
        mixed_rows = jnp.where(first == 0, mixed_rows, jnp.concatenate(halves[::-1], axis=1))

    gain, inverse_gain = norm_gain[0], 1.0 / norm_gain[0]
    weights = route_weight[0, 0]
    coarse = lax.reduce_precision(weights, exponent_bits=8, mantissa_bits=7)
    beside = jnp.pad(jnp.concatenate([coarse, weights - coarse], axis=1), ((0, 0), (0, 126)))
    scaled = jnp.concatenate([mixed_rows * gain, beside], axis=1).astype(jnp.bfloat16)
    packed = jnp.dot(slot_match, scaled, preferred_element_type=jnp.float32).astype(jnp.bfloat16)
    packed = packed.reshape(contexts, per_context, capacity, model_width + 128)
    blocks = [packed[0]] + [shift(packed[k], "ctx", k) for k in range(1, contexts)]
    arrived = jnp.stack([block[..., :model_width] for block in blocks], axis=0)
    weights = jnp.stack([block[..., model_width:] for block in blocks], axis=0)
    weights = weights[..., 0:1].astype(jnp.float32) + weights[..., 1:2].astype(jnp.float32)
    arrived = lax.optimization_barrier(arrived)

    def wanted_by(blocks, exp):
        if per_context == 1:
            return blocks[:, 0]
        return lax.dynamic_index_in_dim(blocks, exp // group_size, 1, keepdims=False)

    hidden_width = down_weight.shape[2]

    def gate_and_up(rows, behind):
        rows = lax.optimization_barrier(rows.reshape(-1, model_width))
        unscaled = rows.astype(jnp.float32) * inverse_gain + behind
        mean_square = jnp.mean(unscaled * unscaled, axis=-1, keepdims=True)
        gate_up = jnp.dot(rows, in_weight[0, 0], preferred_element_type=jnp.float32)
        return gate_up * lax.rsqrt(mean_square + 1e-06)

    def down_part(gate_up):
        hidden = (jax.nn.silu(gate_up[:, :hidden_width]) * gate_up[:, hidden_width:]).astype(
            jnp.bfloat16
        )
        return jnp.dot(hidden, down_weight[0, 0], preferred_element_type=jnp.float32)

    others = [
        shift(wanted_by(arrived, (my_exp + k) % exps), "exp", k) for k in range(1, exps)
    ]
    own_gate_up = lax.optimization_barrier(gate_and_up(wanted_by(arrived, my_exp), 0.0))
    other_gate_up = gate_and_up(jnp.concatenate(others, axis=0), own_gate_up[0, 0] * 0.0)
    other_parts = down_part(other_gate_up).astype(jnp.bfloat16)
    own_part = lax.optimization_barrier(down_part(own_gate_up))
    own_part = own_part.reshape(contexts, capacity, model_width)
    other_parts = other_parts.reshape(exps - 1, contexts, capacity, model_width)
    sums = [0.0] * per_context
    for k in range(exps):
        back = shift(other_parts[k - 1], "exp", -k).astype(jnp.float32) if k else own_part
        if per_context == 1:
            sums[0] = sums[0] + back
        else:
            place = (my_exp + k) % exps // group_size
            sums = [s + jnp.where(place == i, back, 0.0) for i, s in enumerate(sums)]
    finished = arrived.astype(jnp.float32) * inverse_gain + weights * jnp.stack(sums, axis=1)
    finished = finished.astype(jnp.bfloat16)

    def to_next_owner(rows, k):
        pipes = lax.axis_size("pipe")
        pairs = [
            (p * contexts + c, (p + 1) % pipes * contexts + (c - k) % contexts)
            for p in range(pipes)
            for c in range(contexts)
        ]
        return lax.ppermute(rows, ("pipe", "ctx"), pairs)

    returned = [to_next_owner(finished[k], k).reshape(-1, model_width) for k in range(contexts)]
    next_match = (slot_ids[None, :] == next_slots[:, None]).astype(jnp.bfloat16)
    returned = jnp.concatenate(returned, axis=0)
    layer = jnp.dot(next_match, returned, preferred_element_type=jnp.float32)
    return layer.astype(jnp.bfloat16).reshape(1, 1, token_rows, model_width)


def solution(mesh):
    placed = (
        P("pipe", "exp", "ctx", None),
        P("pipe", "exp", "ctx", None),
        P("pipe", "exp", "ctx", None),
        P("pipe", "ctx", "exp"),
        P("pipe", None),
        P("pipe", ("ctx", "exp"), None, None),
        P("pipe", ("ctx", "exp"), None, None),
        P("pipe", "exp", "ctx", None),
        P("pipe", "exp", "ctx", None),
    )
    return jax.shard_map(
        on_device,
        mesh=mesh,
        in_specs=placed,
        out_specs=P("pipe", "exp", "ctx", None),
        check_vma=False,
    )
```

```python
import math

import jax
import jax.numpy as jnp
from jax import lax
from jax.sharding import PartitionSpec as P

QUERY_HEADS = 32
KEY_VALUE_HEADS = 2
HEAD_SIZE = 128


def shift(value, axis, by):
    devices = lax.axis_size(axis)
    return lax.ppermute(value, axis, [(i, (i + by) % devices) for i in range(devices)])


def after(value, *earlier):
    return lax.optimization_barrier((value, *earlier))[0]


def attend_block(query_block, key_rows, value_rows, row_ids, col_ids):
    scores = jnp.einsum(
        "qhd,kd->hqk", query_block, key_rows, preferred_element_type=jnp.float32
    ) * (1.0 / math.sqrt(HEAD_SIZE))
    scores = jnp.where((col_ids[None, :] <= row_ids[:, None])[None, :, :], scores, -jnp.inf)
    attention_weights = jax.nn.softmax(scores, axis=-1).astype(jnp.bfloat16)
    attended = jnp.einsum(
        "hqk,kd->qhd", attention_weights, value_rows, preferred_element_type=jnp.float32
    )
    return attended.astype(jnp.bfloat16)


def mixed_halves(queries, keys_values, residual, out_weight, slots_here):
    contexts, exps = lax.axis_size("ctx"), lax.axis_size("exp")
    me, my_exp = lax.axis_index("ctx"), lax.axis_index("exp")
    rows = queries.shape[0]
    width = residual.shape[1]
    local_heads = QUERY_HEADS // contexts
    group_width = local_heads * HEAD_SIZE

    def pair_for(owner):
        head = owner * local_heads // (QUERY_HEADS // KEY_VALUE_HEADS)
        key = lax.dynamic_slice_in_dim(keys_values, head * HEAD_SIZE, HEAD_SIZE, 1)
        value = lax.dynamic_slice_in_dim(
            keys_values, (KEY_VALUE_HEADS + head) * HEAD_SIZE, HEAD_SIZE, 1
        )
        return jnp.concatenate([key, value], axis=1)

    def queries_for(owner):
        return lax.dynamic_slice_in_dim(queries, owner * group_width, group_width, 1)

    pairs = [pair_for(me)]
    blocks = [queries_for(me)]
    for k in range(1, contexts):
        pairs.append(shift(pair_for((me + k) % contexts), "ctx", k))
    for k in range(1, contexts):
        outgoing = queries_for((me + k) % contexts)
        if k > 1:
            outgoing = after(outgoing, blocks[1])
        blocks.append(shift(outgoing, "ctx", k))
    if exps == 2:
        weights = [out_weight, shift(out_weight, "exp", 1)]
        first = my_exp * (width // 2)
    else:
        gathered = lax.all_gather(out_weight, "exp", axis=1, tiled=True)
        weights = [gathered[:, : width // 2], gathered[:, width // 2 :]]
        first = 0
    offsets = [first, width // 2 - first]

    pair_rows = jnp.concatenate(pairs, axis=0)
    key_rows, value_rows = pair_rows[:, :HEAD_SIZE], pair_rows[:, HEAD_SIZE:]
    within = jnp.arange(rows, dtype=jnp.int32)
    origins = [(me - k) % contexts * rows for k in range(contexts)]
    col_ids = jnp.concatenate([origin + within for origin in origins])

    held, sent, next_slots = [None, None], [], None
    for k in [*range(1, contexts), 0]:
        behind = sum(block[0, 0] * 0.0 for block in sent)
        attended = attend_block(
            (blocks[k] + behind).reshape(rows, local_heads, HEAD_SIZE),
            key_rows,
            value_rows,
            origins[k] + within,
            col_ids,
        ).reshape(rows, group_width)
        if k == contexts - 1:
            next_slots = shift(slots_here + behind, "pipe", 1)
        sent = []
        terms = []
        for half in range(2):
            term = jnp.dot(attended, weights[half], preferred_element_type=jnp.float32)
            if k == 0:
                own = lax.dynamic_slice_in_dim(residual, offsets[half], width // 2, 1)
                term = term + own.astype(jnp.float32)
            if k == 1 and half == 1 and contexts > 2:
                term = term + blocks[2][0, 0].astype(jnp.float32) * 0.0
            terms.append(lax.optimization_barrier(term))
        for half in range(2):
            term = terms[half]
            if held[half] is not None:
                term = term + held[half].astype(jnp.float32)
            if k == 0:
                held[half] = term + next_slots[0, 0] * 0.0
            else:
                sent.append(term.astype(jnp.bfloat16))
                held[half] = shift(sent[half], "ctx", 1)
    return held, first, next_slots[0].astype(jnp.int32)


def on_device(
    queries,
    rotated_keys_values,
    residual,
    out_weight,
    norm_gain,
    in_weight,
    down_weight,
    routes,
    route_weight,
):
    contexts, exps = lax.axis_size("ctx"), lax.axis_size("exp")
    me, my_exp = lax.axis_index("ctx"), lax.axis_index("exp")
    token_rows = queries.shape[2]
    model_width = residual.shape[3]
    group_size = min(4, exps)
    per_context = exps // group_size
    experts = contexts * per_context
    capacity = min(
        token_rows,
        group_size
        * ((3 * token_rows + 2 * experts * group_size - 1) // (2 * experts * group_size)),
    )
    slots = experts * capacity
    expert_ids = routes[0, 0, :, 0]
    expert_hits = (expert_ids[:, None] == jnp.arange(experts, dtype=jnp.int32)[None, :]).astype(
        jnp.int32
    )
    position = jnp.sum((jnp.cumsum(expert_hits, axis=0) - 1) * expert_hits, axis=1)
    distance = (expert_ids // per_context - me) % contexts
    slot_index = (distance * per_context + expert_ids % per_context) * capacity + position
    slot_ids = jnp.arange(slots, dtype=jnp.int32)
    slot_match = (slot_ids[:, None] == slot_index[None, :]).astype(jnp.bfloat16)
    halves, first, next_slots = mixed_halves(
        queries[0, 0],
        rotated_keys_values[0, 0],
        residual[0, 0],
        out_weight[0],
        slot_index.astype(jnp.float32)[None, :],
    )
    mixed_rows = jnp.concatenate(halves, axis=1)
    if exps == 2:
        mixed_rows = jnp.where(first == 0, mixed_rows, jnp.concatenate(halves[::-1], axis=1))

    gain, inverse_gain = norm_gain[0], 1.0 / norm_gain[0]
    weights = route_weight[0, 0]
    coarse = lax.reduce_precision(weights, exponent_bits=8, mantissa_bits=7)
    beside = jnp.pad(jnp.concatenate([coarse, weights - coarse], axis=1), ((0, 0), (0, 126)))
    scaled = jnp.concatenate([mixed_rows * gain, beside], axis=1).astype(jnp.bfloat16)
    packed = jnp.dot(slot_match, scaled, preferred_element_type=jnp.float32).astype(jnp.bfloat16)
    packed = packed.reshape(contexts, per_context, capacity, model_width + 128)
    blocks = [packed[0]] + [shift(packed[k], "ctx", k) for k in range(1, contexts)]
    arrived = jnp.stack([block[..., :model_width] for block in blocks], axis=0)
    weights = jnp.stack([block[..., model_width:] for block in blocks], axis=0)
    weights = weights[..., 0:1].astype(jnp.float32) + weights[..., 1:2].astype(jnp.float32)
    arrived = lax.optimization_barrier(arrived)

    def wanted_by(blocks, exp):
        if per_context == 1:
            return blocks[:, 0]
        return lax.dynamic_index_in_dim(blocks, exp // group_size, 1, keepdims=False)

    hidden_width = down_weight.shape[2]

    def gate_and_up(rows, behind=None):
        rows = lax.optimization_barrier(rows.reshape(-1, model_width))
        unscaled = rows.astype(jnp.float32) * inverse_gain
        if behind is not None:
            lead = behind.shape[0]
            behind = jnp.pad(behind * 0.0, ((0, 0), (0, model_width - behind.shape[1])))
            unscaled = jnp.concatenate([unscaled[:lead] + behind, unscaled[lead:]], axis=0)
        mean_square = jnp.mean(unscaled * unscaled, axis=-1, keepdims=True)
        gate_up = jnp.dot(rows, in_weight[0, 0], preferred_element_type=jnp.float32)
        return gate_up * lax.rsqrt(mean_square + 1e-06)

    def down_part(gate_up, columns):
        hidden = (jax.nn.silu(gate_up[:, :hidden_width]) * gate_up[:, hidden_width:]).astype(
            jnp.bfloat16
        )
        return jnp.dot(hidden, down_weight[0, 0, :, columns], preferred_element_type=jnp.float32)

    others = [
        shift(wanted_by(arrived, (my_exp + k) % exps), "exp", k) for k in range(1, exps)
    ]
    own_gate_up = lax.optimization_barrier(gate_and_up(wanted_by(arrived, my_exp)))
    other_gate_up = gate_and_up(jnp.concatenate(others, axis=0), own_gate_up)
    other_gate_up = lax.optimization_barrier(other_gate_up)

    def to_next_owner(rows, k):
        pipes = lax.axis_size("pipe")
        pairs = [
            (p * contexts + c, (p + 1) % pipes * contexts + (c - k) % contexts)
            for p in range(pipes)
            for c in range(contexts)
        ]
        return lax.ppermute(rows, ("pipe", "ctx"), pairs)

    next_match = (slot_ids[None, :] == next_slots[:, None]).astype(jnp.bfloat16)
    half = model_width // 2
    halves = []
    for columns in (slice(0, half), slice(half, model_width)):
        other_parts = down_part(other_gate_up, columns).astype(jnp.bfloat16)
        other_parts = other_parts.reshape(exps - 1, contexts, capacity, half)
        own_part = lax.optimization_barrier(down_part(own_gate_up, columns))
        own_part = own_part.reshape(contexts, capacity, half)
        sums = [0.0] * per_context
        for k in range(exps):
            back = shift(other_parts[k - 1], "exp", -k).astype(jnp.float32) if k else own_part
            if per_context == 1:
                sums[0] = sums[0] + back
            else:
                place = (my_exp + k) % exps // group_size
                sums = [s + jnp.where(place == i, back, 0.0) for i, s in enumerate(sums)]
        mixed = arrived[..., columns].astype(jnp.float32) * inverse_gain[columns]
        finished = (mixed + weights * jnp.stack(sums, axis=1)).astype(jnp.bfloat16)
        returned = [to_next_owner(finished[k], k).reshape(-1, half) for k in range(contexts)]
        returned = jnp.concatenate(returned, axis=0)
        layer = jnp.dot(next_match, returned, preferred_element_type=jnp.float32)
        halves.append(layer.astype(jnp.bfloat16))
    return jnp.concatenate(halves, axis=1).reshape(1, 1, token_rows, model_width)


def solution(mesh):
    placed = (
        P("pipe", "exp", "ctx", None),
        P("pipe", "exp", "ctx", None),
        P("pipe", "exp", "ctx", None),
        P("pipe", "ctx", "exp"),
        P("pipe", None),
        P("pipe", ("ctx", "exp"), None, None),
        P("pipe", ("ctx", "exp"), None, None),
        P("pipe", "exp", "ctx", None),
        P("pipe", "exp", "ctx", None),
    )
    return jax.shard_map(
        on_device,
        mesh=mesh,
        in_specs=placed,
        out_specs=P("pipe", "exp", "ctx", None),
        check_vma=False,
    )
```

```python
import math

import jax
import jax.numpy as jnp
from jax import lax
from jax.sharding import PartitionSpec as P

QUERY_HEADS = 32
KEY_VALUE_HEADS = 2
HEAD_SIZE = 128


def shift(value, axis, by):
    devices = lax.axis_size(axis)
    return lax.ppermute(value, axis, [(i, (i + by) % devices) for i in range(devices)])


def after(value, *earlier):
    return lax.optimization_barrier((value, *earlier))[0]


def attend_block(query_block, key_rows, value_rows, row_ids, col_ids):
    scores = jnp.einsum(
        "qhd,kd->hqk", query_block, key_rows, preferred_element_type=jnp.float32
    ) * (1.0 / math.sqrt(HEAD_SIZE))
    scores = jnp.where((col_ids[None, :] <= row_ids[:, None])[None, :, :], scores, -jnp.inf)
    attention_weights = jax.nn.softmax(scores, axis=-1).astype(jnp.bfloat16)
    attended = jnp.einsum(
        "hqk,kd->qhd", attention_weights, value_rows, preferred_element_type=jnp.float32
    )
    return attended.astype(jnp.bfloat16)


def mixed_halves(queries, keys_values, residual, out_weight, slots_here):
    contexts, exps = lax.axis_size("ctx"), lax.axis_size("exp")
    me, my_exp = lax.axis_index("ctx"), lax.axis_index("exp")
    rows = queries.shape[0]
    width = residual.shape[1]
    local_heads = QUERY_HEADS // contexts
    group_width = local_heads * HEAD_SIZE

    def pair_for(owner):
        head = owner * local_heads // (QUERY_HEADS // KEY_VALUE_HEADS)
        key = lax.dynamic_slice_in_dim(keys_values, head * HEAD_SIZE, HEAD_SIZE, 1)
        value = lax.dynamic_slice_in_dim(
            keys_values, (KEY_VALUE_HEADS + head) * HEAD_SIZE, HEAD_SIZE, 1
        )
        return jnp.concatenate([key, value], axis=1)

    def queries_for(owner):
        return lax.dynamic_slice_in_dim(queries, owner * group_width, group_width, 1)

    pairs = [pair_for(me)]
    blocks = [queries_for(me)]
    for k in range(1, contexts):
        pairs.append(shift(pair_for((me + k) % contexts), "ctx", k))
    for k in range(1, contexts):
        outgoing = queries_for((me + k) % contexts)
        if k > 1:
            outgoing = after(outgoing, blocks[1])
        blocks.append(shift(outgoing, "ctx", k))
    if exps == 2:
        weights = [out_weight, shift(out_weight, "exp", 1)]
        first = my_exp * (width // 2)
    else:
        gathered = lax.all_gather(out_weight, "exp", axis=1, tiled=True)
        weights = [gathered[:, : width // 2], gathered[:, width // 2 :]]
        first = 0
    offsets = [first, width // 2 - first]

    pair_rows = jnp.concatenate(pairs, axis=0)
    key_rows, value_rows = pair_rows[:, :HEAD_SIZE], pair_rows[:, HEAD_SIZE:]
    within = jnp.arange(rows, dtype=jnp.int32)
    origins = [(me - k) % contexts * rows for k in range(contexts)]
    col_ids = jnp.concatenate([origin + within for origin in origins])

    held, sent, next_slots = [None, None], [], None
    for k in [*range(1, contexts), 0]:
        behind = sum(block[0, 0] * 0.0 for block in sent)
        attended = attend_block(
            (blocks[k] + behind).reshape(rows, local_heads, HEAD_SIZE),
            key_rows,
            value_rows,
            origins[k] + within,
            col_ids,
        ).reshape(rows, group_width)
        if k == contexts - 1:
            next_slots = shift(slots_here + behind, "pipe", 1)
        sent = []
        terms = []
        for half in range(2):
            term = jnp.dot(attended, weights[half], preferred_element_type=jnp.float32)
            if k == 0:
                own = lax.dynamic_slice_in_dim(residual, offsets[half], width // 2, 1)
                term = term + own.astype(jnp.float32)
            if k == 1 and half == 1 and contexts > 2:
                term = term + blocks[2][0, 0].astype(jnp.float32) * 0.0
            terms.append(lax.optimization_barrier(term))
        for half in range(2):
            term = terms[half]
            if held[half] is not None:
                term = term + held[half].astype(jnp.float32)
            if k == 0:
                held[half] = term + next_slots[0, 0] * 0.0
            else:
                sent.append(term.astype(jnp.bfloat16))
                held[half] = shift(sent[half], "ctx", 1)
    return held, first, next_slots[0].astype(jnp.int32)


def on_device(
    queries,
    rotated_keys_values,
    residual,
    out_weight,
    norm_gain,
    in_weight,
    down_weight,
    routes,
    route_weight,
):
    contexts, exps = lax.axis_size("ctx"), lax.axis_size("exp")
    me, my_exp = lax.axis_index("ctx"), lax.axis_index("exp")
    token_rows = queries.shape[2]
    model_width = residual.shape[3]
    group_size = min(4, exps)
    per_context = exps // group_size
    experts = contexts * per_context
    capacity = min(
        token_rows,
        group_size
        * ((3 * token_rows + 2 * experts * group_size - 1) // (2 * experts * group_size)),
    )
    slots = experts * capacity
    expert_ids = routes[0, 0, :, 0]
    expert_hits = (expert_ids[:, None] == jnp.arange(experts, dtype=jnp.int32)[None, :]).astype(
        jnp.int32
    )
    position = jnp.sum((jnp.cumsum(expert_hits, axis=0) - 1) * expert_hits, axis=1)
    distance = (expert_ids // per_context - me) % contexts
    slot_index = (distance * per_context + expert_ids % per_context) * capacity + position
    slot_ids = jnp.arange(slots, dtype=jnp.int32)
    slot_match = (slot_ids[:, None] == slot_index[None, :]).astype(jnp.bfloat16)
    halves, first, next_slots = mixed_halves(
        queries[0, 0],
        rotated_keys_values[0, 0],
        residual[0, 0],
        out_weight[0],
        slot_index.astype(jnp.float32)[None, :],
    )
    mixed_rows = jnp.concatenate(halves, axis=1)
    if exps == 2:
        mixed_rows = jnp.where(first == 0, mixed_rows, jnp.concatenate(halves[::-1], axis=1))

    gain, inverse_gain = norm_gain[0], 1.0 / norm_gain[0]
    weights = route_weight[0, 0]
    coarse = lax.reduce_precision(weights, exponent_bits=8, mantissa_bits=7)
    beside = jnp.pad(jnp.concatenate([coarse, weights - coarse], axis=1), ((0, 0), (0, 126)))
    scaled = jnp.concatenate([mixed_rows * gain, beside], axis=1).astype(jnp.bfloat16)
    packed = jnp.dot(slot_match, scaled, preferred_element_type=jnp.float32).astype(jnp.bfloat16)
    packed = packed.reshape(contexts, per_context, capacity, model_width + 128)
    blocks = [packed[0]] + [shift(packed[k], "ctx", k) for k in range(1, contexts)]
    arrived = jnp.stack([block[..., :model_width] for block in blocks], axis=0)
    weights = jnp.stack([block[..., model_width:] for block in blocks], axis=0)
    weights = weights[..., 0:1].astype(jnp.float32) + weights[..., 1:2].astype(jnp.float32)
    arrived = lax.optimization_barrier(arrived)

    def wanted_by(blocks, exp):
        if per_context == 1:
            return blocks[:, 0]
        return lax.dynamic_index_in_dim(blocks, exp // group_size, 1, keepdims=False)

    hidden_width = down_weight.shape[2]

    def gate_and_up(rows, behind=None):
        rows = lax.optimization_barrier(rows.reshape(-1, model_width))
        unscaled = rows.astype(jnp.float32) * inverse_gain
        if behind is not None:
            lead = behind.shape[0]
            behind = jnp.pad(behind * 0.0, ((0, 0), (0, model_width - behind.shape[1])))
            unscaled = jnp.concatenate([unscaled[:lead] + behind, unscaled[lead:]], axis=0)
        mean_square = jnp.mean(unscaled * unscaled, axis=-1, keepdims=True)
        gate_up = jnp.dot(rows, in_weight[0, 0], preferred_element_type=jnp.float32)
        return gate_up * lax.rsqrt(mean_square + 1e-06)

    def down_part(gate_up, columns):
        hidden = (jax.nn.silu(gate_up[:, :hidden_width]) * gate_up[:, hidden_width:]).astype(
            jnp.bfloat16
        )
        return jnp.dot(hidden, down_weight[0, 0, :, columns], preferred_element_type=jnp.float32)

    others = [
        shift(wanted_by(arrived, (my_exp + k) % exps), "exp", k) for k in range(1, exps)
    ]
    own_gate_up = lax.optimization_barrier(gate_and_up(wanted_by(arrived, my_exp)))
    other_gate_up = gate_and_up(jnp.concatenate(others, axis=0), own_gate_up)
    other_gate_up = lax.optimization_barrier(other_gate_up)

    def to_next_owner(rows, k):
        pipes = lax.axis_size("pipe")
        pairs = [
            (p * contexts + c, (p + 1) % pipes * contexts + (c - k) % contexts)
            for p in range(pipes)
            for c in range(contexts)
        ]
        return lax.ppermute(rows, ("pipe", "ctx"), pairs)

    next_match = (slot_ids[None, :] == next_slots[:, None]).astype(jnp.bfloat16)
    half = model_width // 2
    returned = []
    for columns in (slice(0, half), slice(half, model_width)):
        other_parts = down_part(other_gate_up, columns).astype(jnp.bfloat16)
        other_parts = other_parts.reshape(exps - 1, contexts, capacity, half)
        own_part = lax.optimization_barrier(down_part(own_gate_up, columns))
        own_part = own_part.reshape(contexts, capacity, half)
        sums = [0.0] * per_context
        for k in range(exps):
            back = shift(other_parts[k - 1], "exp", -k).astype(jnp.float32) if k else own_part
            if per_context == 1:
                sums[0] = sums[0] + back
            else:
                place = (my_exp + k) % exps // group_size
                sums = [s + jnp.where(place == i, back, 0.0) for i, s in enumerate(sums)]
        mixed = arrived[..., columns].astype(jnp.float32) * inverse_gain[columns]
        finished = (mixed + weights * jnp.stack(sums, axis=1)).astype(jnp.bfloat16)
        returned.append([to_next_owner(finished[k], k) for k in range(contexts)])
    returned = jnp.concatenate(
        [jnp.concatenate(pair, axis=-1).reshape(-1, model_width) for pair in zip(*returned)], axis=0
    )
    returned = lax.optimization_barrier(returned)
    layer = jnp.dot(next_match, returned, preferred_element_type=jnp.float32)
    return layer.astype(jnp.bfloat16).reshape(1, 1, token_rows, model_width)


def solution(mesh):
    placed = (
        P("pipe", "exp", "ctx", None),
        P("pipe", "exp", "ctx", None),
        P("pipe", "exp", "ctx", None),
        P("pipe", "ctx", "exp"),
        P("pipe", None),
        P("pipe", ("ctx", "exp"), None, None),
        P("pipe", ("ctx", "exp"), None, None),
        P("pipe", "exp", "ctx", None),
        P("pipe", "exp", "ctx", None),
    )
    return jax.shard_map(
        on_device,
        mesh=mesh,
        in_specs=placed,
        out_specs=P("pipe", "exp", "ctx", None),
        check_vma=False,
    )
```

```python
import math

import jax
import jax.numpy as jnp
from jax import lax
from jax.sharding import PartitionSpec as P

QUERY_HEADS = 32
KEY_VALUE_HEADS = 2
HEAD_SIZE = 128


def shift(value, axis, by):
    devices = lax.axis_size(axis)
    return lax.ppermute(value, axis, [(i, (i + by) % devices) for i in range(devices)])


def after(value, *earlier):
    return lax.optimization_barrier((value, *earlier))[0]


def attend_block(query_block, key_rows, value_rows, row_ids, col_ids):
    scores = jnp.einsum(
        "qhd,kd->hqk", query_block, key_rows, preferred_element_type=jnp.float32
    ) * (1.0 / math.sqrt(HEAD_SIZE))
    scores = jnp.where((col_ids[None, :] <= row_ids[:, None])[None, :, :], scores, -jnp.inf)
    attention_weights = jax.nn.softmax(scores, axis=-1).astype(jnp.bfloat16)
    attended = jnp.einsum(
        "hqk,kd->qhd", attention_weights, value_rows, preferred_element_type=jnp.float32
    )
    return attended.astype(jnp.bfloat16)


def mixed_halves(queries, keys_values, residual, out_weight, slots_here):
    contexts, exps = lax.axis_size("ctx"), lax.axis_size("exp")
    me, my_exp = lax.axis_index("ctx"), lax.axis_index("exp")
    rows = queries.shape[0]
    width = residual.shape[1]
    local_heads = QUERY_HEADS // contexts
    group_width = local_heads * HEAD_SIZE

    def pair_for(owner):
        head = owner * local_heads // (QUERY_HEADS // KEY_VALUE_HEADS)
        key = lax.dynamic_slice_in_dim(keys_values, head * HEAD_SIZE, HEAD_SIZE, 1)
        value = lax.dynamic_slice_in_dim(
            keys_values, (KEY_VALUE_HEADS + head) * HEAD_SIZE, HEAD_SIZE, 1
        )
        return jnp.concatenate([key, value], axis=1)

    def queries_for(owner):
        return lax.dynamic_slice_in_dim(queries, owner * group_width, group_width, 1)

    pairs = [pair_for(me)]
    blocks = [queries_for(me)]
    for k in range(1, contexts):
        pairs.append(shift(pair_for((me + k) % contexts), "ctx", k))
    for k in range(1, contexts):
        outgoing = queries_for((me + k) % contexts)
        if k > 1:
            outgoing = after(outgoing, blocks[1])
        blocks.append(shift(outgoing, "ctx", k))
    if exps == 2:
        weights = [out_weight, shift(out_weight, "exp", 1)]
        first = my_exp * (width // 2)
    else:
        gathered = lax.all_gather(out_weight, "exp", axis=1, tiled=True)
        weights = [gathered[:, : width // 2], gathered[:, width // 2 :]]
        first = 0
    offsets = [first, width // 2 - first]

    pair_rows = jnp.concatenate(pairs, axis=0)
    key_rows, value_rows = pair_rows[:, :HEAD_SIZE], pair_rows[:, HEAD_SIZE:]
    within = jnp.arange(rows, dtype=jnp.int32)
    origins = [(me - k) % contexts * rows for k in range(contexts)]
    col_ids = jnp.concatenate([origin + within for origin in origins])

    held, sent, next_slots = [None, None], [], None
    for k in [*range(1, contexts), 0]:
        behind = sum(block[0, 0] * 0.0 for block in sent)
        attended = attend_block(
            (blocks[k] + behind).reshape(rows, local_heads, HEAD_SIZE),
            key_rows,
            value_rows,
            origins[k] + within,
            col_ids,
        ).reshape(rows, group_width)
        if k == contexts - 1:
            next_slots = shift(slots_here + behind, "pipe", 1)
        sent = []
        terms = []
        for half in range(2):
            term = jnp.dot(attended, weights[half], preferred_element_type=jnp.float32)
            if k == 0:
                own = lax.dynamic_slice_in_dim(residual, offsets[half], width // 2, 1)
                term = term + own.astype(jnp.float32)
            if k == 1 and half == 1 and contexts > 2:
                term = term + blocks[2][0, 0].astype(jnp.float32) * 0.0
            terms.append(lax.optimization_barrier(term))
        for half in range(2):
            term = terms[half]
            if held[half] is not None:
                term = term + held[half].astype(jnp.float32)
            if k == 0:
                held[half] = term + next_slots[0, 0] * 0.0
            else:
                sent.append(term.astype(jnp.bfloat16))
                held[half] = shift(sent[half], "ctx", 1)
    return held, first, next_slots[0].astype(jnp.int32)


def on_device(
    queries,
    rotated_keys_values,
    residual,
    out_weight,
    norm_gain,
    in_weight,
    down_weight,
    routes,
    route_weight,
):
    contexts, exps = lax.axis_size("ctx"), lax.axis_size("exp")
    me, my_exp = lax.axis_index("ctx"), lax.axis_index("exp")
    token_rows = queries.shape[2]
    model_width = residual.shape[3]
    group_size = min(4, exps)
    per_context = exps // group_size
    experts = contexts * per_context
    capacity = min(
        token_rows,
        group_size
        * ((3 * token_rows + 2 * experts * group_size - 1) // (2 * experts * group_size)),
    )
    slots = experts * capacity
    expert_ids = routes[0, 0, :, 0]
    expert_hits = (expert_ids[:, None] == jnp.arange(experts, dtype=jnp.int32)[None, :]).astype(
        jnp.int32
    )
    position = jnp.sum((jnp.cumsum(expert_hits, axis=0) - 1) * expert_hits, axis=1)
    distance = (expert_ids // per_context - me) % contexts
    slot_index = (distance * per_context + expert_ids % per_context) * capacity + position
    slot_ids = jnp.arange(slots, dtype=jnp.int32)
    slot_match = (slot_ids[:, None] == slot_index[None, :]).astype(jnp.bfloat16)
    halves, first, next_slots = mixed_halves(
        queries[0, 0],
        rotated_keys_values[0, 0],
        residual[0, 0],
        out_weight[0],
        slot_index.astype(jnp.float32)[None, :],
    )
    mixed_rows = jnp.concatenate(halves, axis=1)
    if exps == 2:
        mixed_rows = jnp.where(first == 0, mixed_rows, jnp.concatenate(halves[::-1], axis=1))

    gain, inverse_gain = norm_gain[0], 1.0 / norm_gain[0]
    weights = route_weight[0, 0]
    coarse = lax.reduce_precision(weights, exponent_bits=8, mantissa_bits=7)
    beside = jnp.pad(jnp.concatenate([coarse, weights - coarse], axis=1), ((0, 0), (0, 126)))
    scaled = jnp.concatenate([mixed_rows * gain, beside], axis=1).astype(jnp.bfloat16)
    packed = jnp.dot(slot_match, scaled, preferred_element_type=jnp.float32).astype(jnp.bfloat16)
    packed = packed.reshape(contexts, per_context, capacity, model_width + 128)
    blocks = [packed[0]] + [shift(packed[k], "ctx", k) for k in range(1, contexts)]
    arrived = jnp.stack([block[..., :model_width] for block in blocks], axis=0)
    weights = jnp.stack([block[..., model_width:] for block in blocks], axis=0)
    weights = weights[..., 0:1].astype(jnp.float32) + weights[..., 1:2].astype(jnp.float32)
    arrived = lax.optimization_barrier(arrived)

    def wanted_by(blocks, exp):
        if per_context == 1:
            return blocks[:, 0]
        return lax.dynamic_index_in_dim(blocks, exp // group_size, 1, keepdims=False)

    hidden_width = down_weight.shape[2]

    def gate_and_up(rows, behind=None):
        rows = lax.optimization_barrier(rows.reshape(-1, model_width))
        unscaled = rows.astype(jnp.float32) * inverse_gain
        if behind is not None:
            lead = behind.shape[0]
            behind = jnp.pad(behind * 0.0, ((0, 0), (0, model_width - behind.shape[1])))
            unscaled = jnp.concatenate([unscaled[:lead] + behind, unscaled[lead:]], axis=0)
        mean_square = jnp.mean(unscaled * unscaled, axis=-1, keepdims=True)
        gate_up = jnp.dot(rows, in_weight[0, 0], preferred_element_type=jnp.float32)
        return gate_up * lax.rsqrt(mean_square + 1e-06)

    def down_part(gate_up):
        hidden = (jax.nn.silu(gate_up[:, :hidden_width]) * gate_up[:, hidden_width:]).astype(
            jnp.bfloat16
        )
        return jnp.dot(hidden, down_weight[0, 0], preferred_element_type=jnp.float32)

    others = [
        shift(wanted_by(arrived, (my_exp + k) % exps), "exp", k) for k in range(1, exps)
    ]
    own_gate_up = lax.optimization_barrier(gate_and_up(wanted_by(arrived, my_exp)))
    other_gate_up = gate_and_up(jnp.concatenate(others, axis=0), own_gate_up[:, :128])
    other_parts = down_part(other_gate_up).astype(jnp.bfloat16)
    own_part = lax.optimization_barrier(down_part(own_gate_up))
    own_part = own_part.reshape(contexts, capacity, model_width)
    other_parts = other_parts.reshape(exps - 1, contexts, capacity, model_width)
    sums = [0.0] * per_context
    for k in range(exps):
        back = shift(other_parts[k - 1], "exp", -k).astype(jnp.float32) if k else own_part
        if per_context == 1:
            sums[0] = sums[0] + back
        else:
            place = (my_exp + k) % exps // group_size
            sums = [s + jnp.where(place == i, back, 0.0) for i, s in enumerate(sums)]
    finished = arrived.astype(jnp.float32) * inverse_gain + weights * jnp.stack(sums, axis=1)
    finished = finished.astype(jnp.bfloat16)

    def to_next_owner(rows, k):
        pipes = lax.axis_size("pipe")
        pairs = [
            (p * contexts + c, (p + 1) % pipes * contexts + (c - k) % contexts)
            for p in range(pipes)
            for c in range(contexts)
        ]
        return lax.ppermute(rows, ("pipe", "ctx"), pairs)

    returned = [to_next_owner(finished[k], k).reshape(-1, model_width) for k in range(contexts)]
    next_match = (slot_ids[None, :] == next_slots[:, None]).astype(jnp.bfloat16)
    returned = jnp.concatenate(returned, axis=0)
    layer = jnp.dot(next_match, returned, preferred_element_type=jnp.float32)
    return layer.astype(jnp.bfloat16).reshape(1, 1, token_rows, model_width)


def solution(mesh):
    placed = (
        P("pipe", "exp", "ctx", None),
        P("pipe", "exp", "ctx", None),
        P("pipe", "exp", "ctx", None),
        P("pipe", "ctx", "exp"),
        P("pipe", None),
        P("pipe", ("ctx", "exp"), None, None),
        P("pipe", ("ctx", "exp"), None, None),
        P("pipe", "exp", "ctx", None),
        P("pipe", "exp", "ctx", None),
    )
    return jax.shard_map(
        on_device,
        mesh=mesh,
        in_specs=placed,
        out_specs=P("pipe", "exp", "ctx", None),
        check_vma=False,
    )
```

```python
import math

import jax
import jax.numpy as jnp
from jax import lax
from jax.sharding import PartitionSpec as P

QUERY_HEADS = 32
KEY_VALUE_HEADS = 2
HEAD_SIZE = 128


def shift(value, axis, by):
    devices = lax.axis_size(axis)
    return lax.ppermute(value, axis, [(i, (i + by) % devices) for i in range(devices)])


def after(value, *earlier):
    return lax.optimization_barrier((value, *earlier))[0]


def attend_block(query_block, key_rows, value_rows, row_ids, col_ids):
    scores = jnp.einsum(
        "qhd,kd->hqk", query_block, key_rows, preferred_element_type=jnp.float32
    ) * (1.0 / math.sqrt(HEAD_SIZE))
    scores = jnp.where((col_ids[None, :] <= row_ids[:, None])[None, :, :], scores, -jnp.inf)
    attention_weights = jax.nn.softmax(scores, axis=-1).astype(jnp.bfloat16)
    attended = jnp.einsum(
        "hqk,kd->qhd", attention_weights, value_rows, preferred_element_type=jnp.float32
    )
    return attended.astype(jnp.bfloat16)


def mixed_halves(queries, keys_values, residual, out_weight, slots_here):
    contexts, exps = lax.axis_size("ctx"), lax.axis_size("exp")
    me, my_exp = lax.axis_index("ctx"), lax.axis_index("exp")
    rows = queries.shape[0]
    width = residual.shape[1]
    local_heads = QUERY_HEADS // contexts
    group_width = local_heads * HEAD_SIZE

    def pair_for(owner):
        head = owner * local_heads // (QUERY_HEADS // KEY_VALUE_HEADS)
        key = lax.dynamic_slice_in_dim(keys_values, head * HEAD_SIZE, HEAD_SIZE, 1)
        value = lax.dynamic_slice_in_dim(
            keys_values, (KEY_VALUE_HEADS + head) * HEAD_SIZE, HEAD_SIZE, 1
        )
        return jnp.concatenate([key, value], axis=1)

    def queries_for(owner):
        return lax.dynamic_slice_in_dim(queries, owner * group_width, group_width, 1)

    pairs = [pair_for(me)]
    blocks = [queries_for(me)]
    for k in range(1, contexts):
        pairs.append(shift(pair_for((me + k) % contexts), "ctx", k))
    for k in range(1, contexts):
        outgoing = queries_for((me + k) % contexts)
        if k > 1:
            outgoing = after(outgoing, blocks[1])
        blocks.append(shift(outgoing, "ctx", k))
    if exps == 2:
        weights = [out_weight, shift(out_weight, "exp", 1)]
        first = my_exp * (width // 2)
    else:
        gathered = lax.all_gather(out_weight, "exp", axis=1, tiled=True)
        weights = [gathered[:, : width // 2], gathered[:, width // 2 :]]
        first = 0
    offsets = [first, width // 2 - first]

    pair_rows = jnp.concatenate(pairs, axis=0)
    key_rows, value_rows = pair_rows[:, :HEAD_SIZE], pair_rows[:, HEAD_SIZE:]
    within = jnp.arange(rows, dtype=jnp.int32)
    origins = [(me - k) % contexts * rows for k in range(contexts)]
    col_ids = jnp.concatenate([origin + within for origin in origins])

    held, sent, next_slots = [None, None], [], None
    for k in [*range(1, contexts), 0]:
        behind = sum(block[0, 0] * 0.0 for block in sent)
        attended = attend_block(
            (blocks[k] + behind).reshape(rows, local_heads, HEAD_SIZE),
            key_rows,
            value_rows,
            origins[k] + within,
            col_ids,
        ).reshape(rows, group_width)
        if k == contexts - 1:
            next_slots = shift(slots_here + behind, "pipe", 1)
        sent = []
        terms = []
        for half in range(2):
            term = jnp.dot(attended, weights[half], preferred_element_type=jnp.float32)
            if k == 0:
                own = lax.dynamic_slice_in_dim(residual, offsets[half], width // 2, 1)
                term = term + own.astype(jnp.float32)
            if k == 1 and half == 0:
                term = term + weights[1][0, 0].astype(jnp.float32) * 0.0
            terms.append(lax.optimization_barrier(term))
        for half in range(2):
            term = terms[half]
            if held[half] is not None:
                term = term + held[half].astype(jnp.float32)
            if k == 0:
                held[half] = term + next_slots[0, 0] * 0.0
            else:
                sent.append(term.astype(jnp.bfloat16))
                held[half] = shift(sent[half], "ctx", 1)
    return held, first, next_slots[0].astype(jnp.int32)


def on_device(
    queries,
    rotated_keys_values,
    residual,
    out_weight,
    norm_gain,
    in_weight,
    down_weight,
    routes,
    route_weight,
):
    contexts, exps = lax.axis_size("ctx"), lax.axis_size("exp")
    me, my_exp = lax.axis_index("ctx"), lax.axis_index("exp")
    token_rows = queries.shape[2]
    model_width = residual.shape[3]
    group_size = min(4, exps)
    per_context = exps // group_size
    experts = contexts * per_context
    capacity = min(
        token_rows,
        group_size
        * ((3 * token_rows + 2 * experts * group_size - 1) // (2 * experts * group_size)),
    )
    slots = experts * capacity
    expert_ids = routes[0, 0, :, 0]
    expert_hits = (expert_ids[:, None] == jnp.arange(experts, dtype=jnp.int32)[None, :]).astype(
        jnp.int32
    )
    position = jnp.sum((jnp.cumsum(expert_hits, axis=0) - 1) * expert_hits, axis=1)
    distance = (expert_ids // per_context - me) % contexts
    slot_index = (distance * per_context + expert_ids % per_context) * capacity + position
    slot_ids = jnp.arange(slots, dtype=jnp.int32)
    slot_match = (slot_ids[:, None] == slot_index[None, :]).astype(jnp.bfloat16)
    halves, first, next_slots = mixed_halves(
        queries[0, 0],
        rotated_keys_values[0, 0],
        residual[0, 0],
        out_weight[0],
        slot_index.astype(jnp.float32)[None, :],
    )
    mixed_rows = jnp.concatenate(halves, axis=1)
    if exps == 2:
        mixed_rows = jnp.where(first == 0, mixed_rows, jnp.concatenate(halves[::-1], axis=1))

    gain, inverse_gain = norm_gain[0], 1.0 / norm_gain[0]
    weights = route_weight[0, 0]
    coarse = lax.reduce_precision(weights, exponent_bits=8, mantissa_bits=7)
    beside = jnp.pad(jnp.concatenate([coarse, weights - coarse], axis=1), ((0, 0), (0, 126)))
    scaled = jnp.concatenate([mixed_rows * gain, beside], axis=1).astype(jnp.bfloat16)
    packed = jnp.dot(slot_match, scaled, preferred_element_type=jnp.float32).astype(jnp.bfloat16)
    packed = packed.reshape(contexts, per_context, capacity, model_width + 128)
    blocks = [packed[0]] + [shift(packed[k], "ctx", k) for k in range(1, contexts)]
    arrived = jnp.stack([block[..., :model_width] for block in blocks], axis=0)
    weights = jnp.stack([block[..., model_width:] for block in blocks], axis=0)
    weights = weights[..., 0:1].astype(jnp.float32) + weights[..., 1:2].astype(jnp.float32)
    arrived = lax.optimization_barrier(arrived)

    def wanted_by(blocks, exp):
        if per_context == 1:
            return blocks[:, 0]
        return lax.dynamic_index_in_dim(blocks, exp // group_size, 1, keepdims=False)

    hidden_width = down_weight.shape[2]

    def gate_and_up(rows, behind=None):
        rows = lax.optimization_barrier(rows.reshape(-1, model_width))
        unscaled = rows.astype(jnp.float32) * inverse_gain
        if behind is not None:
            lead = behind.shape[0]
            behind = jnp.pad(behind * 0.0, ((0, 0), (0, model_width - behind.shape[1])))
            unscaled = jnp.concatenate([unscaled[:lead] + behind, unscaled[lead:]], axis=0)
        mean_square = jnp.mean(unscaled * unscaled, axis=-1, keepdims=True)
        gate_up = jnp.dot(rows, in_weight[0, 0], preferred_element_type=jnp.float32)
        return gate_up * lax.rsqrt(mean_square + 1e-06)

    def down_part(gate_up):
        hidden = (jax.nn.silu(gate_up[:, :hidden_width]) * gate_up[:, hidden_width:]).astype(
            jnp.bfloat16
        )
        return jnp.dot(hidden, down_weight[0, 0], preferred_element_type=jnp.float32)

    others = [
        shift(wanted_by(arrived, (my_exp + k) % exps), "exp", k) for k in range(1, exps)
    ]
    own_gate_up = lax.optimization_barrier(gate_and_up(wanted_by(arrived, my_exp)))
    other_gate_up = gate_and_up(jnp.concatenate(others, axis=0), own_gate_up[:, :128])
    other_parts = down_part(other_gate_up).astype(jnp.bfloat16)
    own_part = lax.optimization_barrier(down_part(own_gate_up))
    own_part = own_part.reshape(contexts, capacity, model_width)
    other_parts = other_parts.reshape(exps - 1, contexts, capacity, model_width)
    sums = [0.0] * per_context
    for k in range(exps):
        back = shift(other_parts[k - 1], "exp", -k).astype(jnp.float32) if k else own_part
        if per_context == 1:
            sums[0] = sums[0] + back
        else:
            place = (my_exp + k) % exps // group_size
            sums = [s + jnp.where(place == i, back, 0.0) for i, s in enumerate(sums)]
    finished = arrived.astype(jnp.float32) * inverse_gain + weights * jnp.stack(sums, axis=1)
    finished = finished.astype(jnp.bfloat16)

    def to_next_owner(rows, k):
        pipes = lax.axis_size("pipe")
        pairs = [
            (p * contexts + c, (p + 1) % pipes * contexts + (c - k) % contexts)
            for p in range(pipes)
            for c in range(contexts)
        ]
        return lax.ppermute(rows, ("pipe", "ctx"), pairs)

    returned = [to_next_owner(finished[k], k).reshape(-1, model_width) for k in range(contexts)]
    next_match = (slot_ids[None, :] == next_slots[:, None]).astype(jnp.bfloat16)
    returned = jnp.concatenate(returned, axis=0)
    layer = jnp.dot(next_match, returned, preferred_element_type=jnp.float32)
    return layer.astype(jnp.bfloat16).reshape(1, 1, token_rows, model_width)


def solution(mesh):
    placed = (
        P("pipe", "exp", "ctx", None),
        P("pipe", "exp", "ctx", None),
        P("pipe", "exp", "ctx", None),
        P("pipe", "ctx", "exp"),
        P("pipe", None),
        P("pipe", ("ctx", "exp"), None, None),
        P("pipe", ("ctx", "exp"), None, None),
        P("pipe", "exp", "ctx", None),
        P("pipe", "exp", "ctx", None),
    )
    return jax.shard_map(
        on_device,
        mesh=mesh,
        in_specs=placed,
        out_specs=P("pipe", "exp", "ctx", None),
        check_vma=False,
    )
```
